128 devices in a mesh: gx: 16 (over x_hi, y, core), gz: 8 (over x_lo, z).
Axes of the slice: x: 4 (x_hi: 2, x_lo: 2; x = x_hi * 2 + x_lo), y: 4, z: 4, core: 2. Of those that a mesh axis runs over, the one named last changes fastest.
Arguments:
- right_side: float32 [256, 512, 1024], P('gx', None, 'gz'), may hold values from -8 to 8
- pressure: float32 [256, 512, 1024], P('gx', None, 'gz'), may hold values from -8 to 8
- diagonal: float32 [256, 512, 1024], P('gx', None, 'gz'), may hold values from 0.05 to 4
- corrections: float32 [32768, 128], P(('gx', 'gz')), may hold values from -6 to 6
- wall_cells: int32 [32768, 128], P(('gx', 'gz')), may hold values from 0 to 4095
- owners: int32 [32768, 1], P(('gx', 'gz')), may hold values from 0 to 127; in each aligned block of 256 rows (0 to 255, 256 to 511, ...) at most 4 rows name the same one
Outputs:
- updated: float32 [256, 512, 1024], P('gx', None, 'gz')
The draws below stay inside these ranges and needn't reach their ends.
Inputs may be any that keep to these rules, and one draw needn't show every extreme that they name: `owners`: among the rows of one device no owner is named by more than 4 rows, a bound that some block reaches. `wall_cells`: index plane * 16 * 128 + x * 128 + z of a wall cell in the owner's block.
All inputs are finite; a program needn't handle non-finite values.
Results may differ from the reference program's by a relative error of at most 0.0003.
Values sent between devices are 32-bit elements; how exact they have to be, the bound alone decides.
No kernel may reach another device: no remote copies, remote signals or barrier semaphores. Data moves between devices by JAX's collectives and lax.ppermute only.
A program may use at most 192 MiB of HBM per device.

```python
import math
import jax
import jax.numpy as jnp
import numpy as np
from jax import lax

CX = 16
NY = 512
CZ = 128
INTERSECTION = 2
JSTEPS = 4
BLK_DEV = 256
BLOCK_LEN = 128
CAP = 4
NX = 256
NZ = 1024
BLOCKS = 32768
N_GX = 16
N_GZ = 8


def set_ends(entries, stream_key, low, largest):
    place = [jax.random.randint(jax.random.fold_in(stream_key, axis), (), 0, length) for axis, length in enumerate(entries.shape)]
    main_axis = entries.shape.index(max(entries.shape))
    next_to = place[:main_axis] + [(place[main_axis] + 1) % entries.shape[main_axis]] + place[main_axis + 1:]
    return entries.at[tuple(place)].set(low).at[tuple(next_to)].set(largest)


def shard_levels(own_key, extent, cuts, least, top_value):
    def one(axis_at, parts):
        steps = jax.random.uniform(jax.random.fold_in(jax.random.fold_in(own_key, 6), axis_at), (parts,), jnp.float32, least / len(cuts), top_value / len(cuts))
        return jnp.repeat(jnp.exp(steps), extent[axis_at] // parts).reshape((-1,) + (1,) * (len(extent) - axis_at - 1))

    factor_of = one(*cuts[0])
    for cut in cuts[1:]:
        factor_of = factor_of * one(*cut)
    return factor_of


def shared_out(stream_key, own, number, rows, number_of, top, bound, skew):
    order = jax.random.permutation(stream_key, number_of)
    heavy_load, common = load_shares(number_of, rows * top, bound, skew, True), load_shares(number_of, rows * top, bound, skew, False)
    places = jnp.arange(number_of)

    def named(tallies, rotation):
        used = int((tallies > 0).sum())
        fixed = max(1, used // 4)
        passed = fixed + (places - fixed + rotation * (used - fixed)) % max(1, number_of - fixed)
        return jnp.zeros((number_of,), jnp.int32).at[order[jnp.where(places < fixed, places, passed)]].set(jnp.asarray(tallies, jnp.int32))

    tallies = jnp.where(number % 4 == 0, named(heavy_load, number // 4), named(common, number - number // 4 - 1))
    mixed = jax.random.permutation(jax.random.fold_in(own, 3), number_of)
    source_of, taker = mixed[0:number_of // 2 * 2:2], mixed[1:number_of // 2 * 2:2]
    room = jnp.minimum(tallies[source_of] - 1, bound - tallies[taker]) // 2
    room = jnp.where((source_of == order[0]) | (taker == order[0]) | (tallies[taker] == 0), 0, jnp.maximum(room, 0))
    passed = jax.random.randint(jax.random.fold_in(own, 4), (number_of // 2,), 0, 1 << 20) % (room + 1)
    tallies = tallies.at[source_of].add(-passed).at[taker].add(passed)
    members = jnp.searchsorted(jnp.cumsum(tallies), jnp.arange(rows * top), side="right").astype(jnp.int32)
    table = members.reshape(top, rows).T
    table = table[jax.random.permutation(jax.random.fold_in(own, 1), rows)]
    rotation = jax.random.randint(jax.random.fold_in(own, 2), (rows, 1), 0, top)
    return jnp.take_along_axis(table, (jnp.arange(top)[None, :] + rotation) % top, axis=1)


def load_shares(amount, total, reach, skew, full):
    portions = [(1 << 20) // math.isqrt(standing ** skew) + 1 for standing in range(1, amount + 1)]
    largest = reach if full else min(reach, max(-(-total // amount), total * portions[0] // sum(portions)))
    least = 1 if total - largest >= amount - 1 else 0
    holding, spare = [largest] + [least] * (amount - 1), total - largest - least * (amount - 1)
    while spare > 0:
        free = [i for i in range(1, amount) if holding[i] < largest] or [i for i in range(1, amount) if holding[i] < reach]
        whole, left = sum([portions[i] for i in free]), spare
        for i in free:
            more = min(reach - holding[i], max(1, left * portions[i] // whole), spare)
            holding[i] = holding[i] + more
            spare = spare - more
    return np.array(holding)


def normal_values(own_key, shape, deviation, reach, cuts=(), held_as=jnp.bfloat16):
    loudness = shard_levels(own_key, shape, cuts, -0.22, 0.18) if cuts else 1.0
    values = jax.random.normal(own_key, shape, jnp.float32) * deviation * loudness
    return jnp.minimum(jnp.maximum(values, -reach), reach).astype(held_as)


def setup_inputs(seed: int = 0) -> dict:
    splits = jax.random.split(jax.random.key(seed), 7)
    right_side = normal_values(splits[0], (NX, NY, NZ), 1.0, 8.0, ((0, 16), (2, 8)), jnp.float32)
    pressure = normal_values(splits[1], (NX, NY, NZ), 1.0, 8.0, ((0, 16), (2, 8)), jnp.float32)
    diagonal = jnp.clip(jnp.exp(math.log(4.0) - 4.3820266 * jax.random.uniform(splits[2], (NX, NY, NZ), jnp.float32) ** shard_levels(splits[2], (NX, NY, NZ), ((0, 16), (2, 8)), -0.2, 0.2)), 0.05, 4.0)
    corrections = normal_values(splits[3], (BLOCKS, BLOCK_LEN), 1.0, 6.0, ((0, 128),), jnp.float32)
    wall_cells = set_ends(jax.random.randint(splits[4], (BLOCKS, BLOCK_LEN), 0, 2 * CX * CZ), jax.random.fold_in(splits[4], 1), 0, (2 * CX * CZ) - 1).astype(jnp.int32)
    owners_keys = jax.random.split(jax.random.fold_in(splits[5], 1), BLOCKS // BLK_DEV)
    owners_turns = jax.random.permutation(jax.random.fold_in(splits[5], 3), BLOCKS // BLK_DEV)
    owners = jax.vmap(lambda own, number: shared_out(jax.random.fold_in(splits[5], 2), own, number, BLK_DEV, N_GX * N_GZ, 1, CAP, 2))(owners_keys, owners_turns).reshape((BLOCKS, 1))
    return {"right_side": right_side, "pressure": pressure, "diagonal": diagonal, "corrections": corrections, "wall_cells": wall_cells, "owners": owners}


def reference(right_side, pressure, diagonal, corrections, wall_cells, owners):
    own = owners[:, 0]
    slab_index = own // N_GZ
    span_index = own % N_GZ
    plane = wall_cells // (CX * CZ)
    rest = wall_cells % (CX * CZ)
    xcell = slab_index[:, None] * CX + rest // CZ
    zcell = span_index[:, None] * CZ + rest % CZ
    flat = ((plane * NX + xcell) * NZ + zcell).astype(jnp.int32)
    wall = jnp.zeros((2 * NX * NZ,), jnp.float32).at[flat.ravel()].add(corrections.ravel()).reshape(2, NX, NZ)
    source = right_side.at[:, 0, :].add(wall[0]).at[:, NY - 1, :].add(wall[1])
    ypad = jnp.pad(pressure, ((0, 0), (1, 1), (0, 0)))
    beside = jnp.roll(pressure, 1, 0) + jnp.roll(pressure, -1, 0)
    beside = beside + ypad[:, 2:, :] + ypad[:, :-2, :]
    beside = beside + jnp.roll(pressure, 1, 2) + jnp.roll(pressure, -1, 2)
    res = source - ((6.0 + diagonal) * pressure - beside)

    def slab(s):
        index = ((s * CX - INTERSECTION + jnp.arange(CX + 2 * INTERSECTION, dtype=jnp.int32)) % NX).astype(jnp.int32)
        r_ext = jnp.take(res, index, axis=0)
        dg = 6.0 + jnp.take(diagonal, index, axis=0)
        e = 0.8 * r_ext / dg
        for step in range(JSTEPS - 1):
            padded = jnp.pad(e, ((1, 1), (1, 1), (0, 0)))
            near = padded[2:, 1:-1, :] + padded[:-2, 1:-1, :]
            near = near + padded[1:-1, 2:, :] + padded[1:-1, :-2, :]
            near = near + jnp.roll(e, 1, 2) + jnp.roll(e, -1, 2)
            e = e + 0.8 * (r_ext - dg * e + near) / dg
        return e[INTERSECTION:INTERSECTION + CX]

    corr = lax.map(slab, jnp.arange(N_GX, dtype=jnp.int32)).reshape(NX, NY, NZ)
    return pressure + corr
```

```python
import jax
import jax.numpy as jnp
from jax import lax
from jax.experimental import pallas as pl
from jax.experimental.pallas import tpu as pltpu
from jax.sharding import PartitionSpec as P

F32 = jnp.float32
BF16 = jnp.bfloat16
AXES = ("gx", "gz")
VMEM = pl.BlockSpec(memory_space=pltpu.VMEM)
HBM = pl.BlockSpec(memory_space=pl.ANY)
MIB = 2**20


def sds(*shape):
    return jax.ShapeDtypeStruct(shape, F32)


def params(mib):
    return pltpu.CompilerParams(vmem_limit_bytes=mib * MIB)


def cost(us):
    return pl.CostEstimate(flops=0, transcendentals=0, bytes_accessed=us * 3_000_000)


def gain(diag):
    return 0.8 / (6.0 + diag)


def pack_kernel(corr_ref, cell_ref, own_ref, out_ref):
    blocks = corr_ref.shape[0]
    rows = out_ref.shape[0]
    own_row = own_ref[...].astype(F32)
    row = lax.broadcasted_iota(jnp.int32, (blocks, blocks), 0)
    col = lax.broadcasted_iota(jnp.int32, (blocks, blocks), 1)
    own = jnp.sum(jnp.where(row == col, own_row, 0.0), axis=1, keepdims=True)
    same = jnp.where((own == own_row) & (row < col), 1.0, 0.0)
    slot = own_row * 8.0 + jnp.sum(same, axis=0, keepdims=True)
    index = lax.broadcasted_iota(jnp.int32, (rows, blocks), 0).astype(F32)
    put_v = jnp.where(index == slot, 1.0, 0.0).astype(BF16)
    put_c = jnp.where(index == slot + 4.0, 1.0, 0.0).astype(BF16)
    vals = corr_ref[...]
    high = vals.astype(BF16)
    rest = vals - high.astype(F32)
    mid = rest.astype(BF16)
    low = (rest - mid.astype(F32)).astype(BF16)
    cells = cell_ref[...]
    major = (cells // 128).astype(F32).astype(BF16)
    minor = (cells % 128).astype(F32).astype(BF16)

    def put(place, what):
        return jnp.dot(place, what, preferred_element_type=F32)

    sent = put(put_v, high) + put(put_v, mid) + put(put_v, low)
    out_ref[...] = sent + (put(put_c, major) * 128.0 + put(put_c, minor))


def pack(corrections, wall_cells, owners, n_dev):
    return pl.pallas_call(
        pack_kernel,
        out_shape=sds(n_dev * 8, corrections.shape[1]),
        in_specs=[VMEM] * 3,
        out_specs=VMEM,
        compiler_params=params(56),
        cost_estimate=cost(3),
    )(corrections, wall_cells, owners.reshape(1, -1))


def wall_kernel(got_ref, after_ref, w_ref, high_s, low_s, major_s, minor_s):
    rows = got_ref.shape[0]
    got = got_ref[...]
    high = got.astype(BF16).astype(F32)
    high_s[...] = high
    low_s[...] = got - high
    major = jnp.floor(got * (1.0 / 128.0))
    major_s[...] = major
    minor_s[...] = got - major * 128.0
    many = 8
    row_id = lax.broadcasted_iota(jnp.int32, (32, 128), 0).astype(F32)
    col_id = lax.broadcasted_iota(jnp.int32, (128, 128), 0).astype(F32)

    def spread(ref, at, n):
        return jnp.broadcast_to(ref[pl.ds(at, 1), :], (n, 128))

    def step(i, total):
        lefts, rights = [], []
        for k in range(many):
            at = i * (2 * many) + (k // 4) * 8 + k % 4
            hit = spread(major_s, at + 4, 32) == row_id
            top = jnp.where(hit, spread(high_s, at, 32), 0.0).astype(BF16)
            end = jnp.where(hit, spread(low_s, at, 32), 0.0).astype(BF16)
            lefts.append(jnp.concatenate([top, end], axis=0))
            hot = spread(minor_s, at + 4, 128) == col_id
            rights.append(jnp.where(hot, 1.0, 0.0).astype(BF16))
        left = jnp.concatenate(lefts, axis=1)
        right = jnp.concatenate(rights, axis=1)
        return total + lax.dot_general(
            left, right, (((1,), (1,)), ((), ())), preferred_element_type=F32
        )

    total = lax.fori_loop(0, rows // (2 * many), step, jnp.zeros((64, 128), F32), unroll=8)
    w_ref[...] = total[:32] + total[32:]


def wall_sums(got, after):
    scratch = [pltpu.VMEM(got.shape, F32)] * 4
    return pl.pallas_call(
        wall_kernel,
        out_shape=sds(32, 128),
        in_specs=[VMEM, HBM],
        out_specs=VMEM,
        scratch_shapes=scratch,
        compiler_params=params(16),
        cost_estimate=cost(7),
    )(got, after)


def edge_kernel(p_ref, pu_ref, pd_ref, r_ref, d_ref, after_ref, zl_ref, zr_ref, dx_ref, xl_ref, xr_ref, pk_s, t_s):
    i = pl.program_id(0)
    lane = lax.broadcasted_iota(jnp.int32, (32, 128), 1)
    small = 640
    base = 0
    for which, (ref, depth) in enumerate(((p_ref, 4), (r_ref, 3), (d_ref, 3))):
        for sub in range(4):
            acc = None
            for x in range(16):
                moved = pltpu.roll(ref[x, sub * 32 : sub * 32 + 32, :], (x * 8 + 4) % 128, 1)
                acc = moved if acc is None else jnp.where(lane // 8 == x, moved, acc)
            pk_s[which, sub * 32 : sub * 32 + 32, :] = acc
        t_s[which] = pk_s[which].T
        for k in range(4):
            left = t_s[which, pl.ds(4 + k, 16, stride=8), :]
            right = t_s[which, pl.ds(3 - k, 16, stride=8), :]
            if k < depth:
                q = base + k
                zl_ref[q * 16 : q * 16 + 16, :] = left
                zr_ref[q * 16 : q * 16 + 16, :] = right
                for side, v in enumerate((left, right)):
                    at = small + side * 32 + q * 3
                    xl_ref[0, at : at + 3, :] = v[0:3]
                    xr_ref[0, at : at + 3, :] = v[13:16]
            elif which == 2:
                dx_ref[0] = left
                dx_ref[1] = right
        base += depth

    row = lax.broadcasted_iota(jnp.int32, (128, 128), 0)
    col = lax.broadcasted_iota(jnp.int32, (128, 128), 1)
    first = jnp.where(i > 0, 1.0, 0.0)
    last = jnp.where(i < pl.num_programs(0) - 1, 1.0, 0.0)

    def level0(x, nbrs):
        mine = p_ref[x]
        up = jnp.where(row == 0, pu_ref[x, 7:8, :] * first, pltpu.roll(mine, 1, 0))
        down = jnp.where(row == 127, pd_ref[x, 0:1, :] * last, pltpu.roll(mine, 127, 0))
        near = up + down
        near = near + jnp.where(col == 0, 0.0, pltpu.roll(mine, 1, 1))
        near = near + jnp.where(col == 127, 0.0, pltpu.roll(mine, 127, 1))
        for n in nbrs:
            near = near + p_ref[n]
        g = gain(d_ref[x])
        return g * (r_ref[x] + near) - 0.8 * mine, g

    for ref, edge, inner, third in ((xl_ref, 0, 1, 2), (xr_ref, 15, 14, 13)):
        ref[0, 0:128, :] = p_ref[edge]
        e, g = level0(edge, (inner,))
        ref[0, 128:256, :] = e
        ref[0, 384:512, :] = g
        e, g = level0(inner, (edge, third))
        ref[0, 256:384, :] = e
        ref[0, 512:640, :] = g
        for side in range(2):
            ref[0, small + side * 32 + 30 : small + side * 32 + 32, :] = jnp.zeros((2, 128), F32)


def edges(p, r, d, after):
    nx, ny, nz = p.shape
    whole = pl.BlockSpec((nx, 128, 128), lambda i: (0, i, 0))
    above = pl.BlockSpec((nx, 8, 128), lambda i: (0, jnp.maximum(16 * i - 1, 0), 0))
    under = pl.BlockSpec((nx, 8, 128), lambda i: (0, jnp.minimum(16 * i + 16, ny // 8 - 1), 0))
    strip = pl.BlockSpec((160, 128), lambda i: (0, i))
    return pl.pallas_call(
        edge_kernel,
        grid=(ny // 128,),
        in_specs=[whole, above, under, whole, whole, HBM],
        out_specs=[
            strip,
            strip,
            pl.BlockSpec((2, nx, 128), lambda i: (0, 0, i)),
            pl.BlockSpec((1, 704, nz), lambda i: (i, 0, 0)),
            pl.BlockSpec((1, 704, nz), lambda i: (i, 0, 0)),
        ],
        out_shape=[sds(224, ny), sds(224, ny), sds(2, nx, ny), sds(ny // 128, 704, nz), sds(ny // 128, 704, nz)],
        scratch_shapes=[pltpu.VMEM((3, 128, 128), F32), pltpu.VMEM((3, 128, 128), F32)],
        compiler_params=params(56),
        cost_estimate=cost(9),
    )(p, p, p, r, d, after)


def relay_kernel(zl_in, zr_in, xp_ref, xn_ref, after_ref, zl_ref, zr_ref, sem):
    copies = []
    for side, z in enumerate((zl_ref, zr_ref)):
        for k, x in enumerate((xp_ref, xn_ref)):
            for b in range(x.shape[0]):
                at = 640 + side * 32
                lanes = z.at[160 + 32 * k : 192 + 32 * k, b * 128 : b * 128 + 128]
                copies.append(pltpu.make_async_copy(x.at[b, at : at + 32, :], lanes, sem.at[len(copies)]))
    for c in copies:
        c.start()
    for c in copies:
        c.wait()


def relay(zl, zr, x_prev, x_next, after):
    return pl.pallas_call(
        relay_kernel,
        out_shape=[sds(*zl.shape), sds(*zr.shape)],
        in_specs=[HBM] * 5,
        out_specs=[HBM] * 2,
        scratch_shapes=[pltpu.SemaphoreType.DMA((4 * x_prev.shape[0],))],
        input_output_aliases={0: 0, 1: 1},
        compiler_params=params(4),
        cost_estimate=cost(1),
    )(zl, zr, x_prev, x_next, after)


CH = 64


def span(mine):
    col = lax.broadcasted_iota(jnp.int32, mine.shape, 1)
    near = jnp.where(col == 0, 0.0, pltpu.roll(mine, 1, 1))
    return near + jnp.where(col == mine.shape[1] - 1, 0.0, pltpu.roll(mine, mine.shape[1] - 1, 1))


def beside(n):
    a = lax.broadcasted_iota(jnp.int32, (2 * n, n), 0) % n
    b = lax.broadcasted_iota(jnp.int32, (2 * n, n), 1)
    return jnp.where((a == b + 1) | (a == b - 1), 1.0, 0.0).astype(BF16)


def spans(v, place):
    high = v.astype(BF16)
    low = (v - high.astype(F32)).astype(BF16)
    return jnp.dot(jnp.concatenate([high, low], axis=1), place, preferred_element_type=F32)


def main_kernel(p_hbm, r_hbm, d_hbm, after_ref, out_hbm, e1_hbm, token_ref, p_s, g_s, e0_s, e1_s, e2_s, p_sem, r_sem, d_sem, o_sem, e_sem):
    nx, ny, nz = p_hbm.shape
    chunks = ny // CH

    def rows(c):
        return pl.ds(pl.multiple_of(c * CH, CH), CH)

    def held(c):
        return pl.ds(pl.multiple_of(8 + c * CH, 8), CH)

    def p_copy(c):
        return pltpu.make_async_copy(p_hbm.at[:, rows(c), :], p_s.at[:, held(c), :], p_sem.at[c])

    def r_copy(c):
        return pltpu.make_async_copy(r_hbm.at[:, rows(c), :], e0_s.at[:, held(c), :], r_sem.at[c])

    def d_copy(c):
        return pltpu.make_async_copy(d_hbm.at[:, rows(c), :], g_s.at[:, rows(c), :], d_sem.at[c])

    def o_copy(c):
        return pltpu.make_async_copy(p_s.at[:, held(c), :], out_hbm.at[:, rows(c), :], o_sem.at[c])

    p_copy(0).start()
    for c in range(chunks):
        r_copy(c).start()
        d_copy(c).start()
        if c + 1 < chunks:
            p_copy(c + 1).start()
    for ref in (p_s, e0_s, e1_s, e2_s):
        for x in range(nx):
            ref[x, 0:8, :] = jnp.zeros((8, nz), F32)
            ref[x, ny + 8 : ny + 16, :] = jnp.zeros((8, nz), F32)
    token_ref[...] = jnp.zeros(token_ref.shape, F32)
    nothing = jnp.zeros((CH, nz), F32)
    place = beside(nz)
    half = nx // 2

    def sweep(src, c, update):
        start = c * CH + 8
        here = pl.ds(pl.multiple_of(start, 8), CH)
        even = jnp.concatenate([src[2 * q, here, :] for q in range(half)], axis=0)
        sums = spans(even, place).reshape(half, CH, nz)
        before, mine = nothing, src[0, here, :]
        for x in range(nx):
            after = src[x + 1, here, :] if x + 1 < nx else nothing
            near = before + after + src[x, pl.ds(start - 1, CH), :] + src[x, pl.ds(start + 1, CH), :]
            update(x, mine, near + (sums[x // 2] if x % 2 == 0 else span(mine)), here)
            before, mine = mine, after

    p_copy(0).wait()

    def level0(c, carry):
        @pl.when(c + 1 < chunks)
        def _():
            p_copy(c + 1).wait()

        r_copy(c).wait()
        d_copy(c).wait()
        here_g = rows(c)

        def update(x, mine, near, here):
            g = gain(g_s[x, here_g, :])
            g_s[x, here_g, :] = g
            e0_s[x, here, :] = g * (e0_s[x, here, :] + near) - 0.8 * mine

        sweep(p_s, c, update)
        return carry

    lax.fori_loop(0, chunks, level0, 0)

    def level1(c, carry):
        here_g = rows(c)

        def update(x, mine, near, here):
            e1_s[x, here, :] = 1.2 * mine + g_s[x, here_g, :] * near

        sweep(e0_s, c, update)
        return carry

    lax.fori_loop(0, chunks, level1, 0)
    sent = [pltpu.make_async_copy(e1_s.at[x, pl.ds(8, ny), :], e1_hbm.at[k], e_sem.at[k]) for k, x in enumerate((0, nx - 1))]
    for s in sent:
        s.start()

    def level2(c, carry):
        here_g = rows(c)

        def update(x, mine, near, here):
            e2_s[x, here, :] = 0.2 * mine + e0_s[x, here, :] + g_s[x, here_g, :] * near

        sweep(e1_s, c, update)
        return carry

    lax.fori_loop(0, chunks, level2, 0)

    def level3(c, carry):
        here_g = rows(c)

        def update(x, mine, near, here):
            e3 = 0.2 * mine + e0_s[x, here, :] + g_s[x, here_g, :] * near
            p_s[x, here, :] = p_s[x, here, :] + e3

        sweep(e2_s, c, update)
        o_copy(c).start()
        return carry

    lax.fori_loop(0, chunks, level3, 0)
    for s in sent:
        s.wait()
    for c in range(chunks):
        o_copy(c).wait()


def main_part(p, r, d, after):
    nx, ny, nz = p.shape
    chunks = ny // CH
    tall = pltpu.VMEM((nx, ny + 16, nz), F32)
    dma = pltpu.SemaphoreType.DMA
    return pl.pallas_call(
        main_kernel,
        out_shape=[sds(nx, ny, nz), sds(2, ny, nz), sds(8, 128)],
        in_specs=[HBM] * 4,
        out_specs=[HBM, HBM, VMEM],
        scratch_shapes=[tall, pltpu.VMEM((nx, ny, nz), F32), tall, tall, tall, dma((chunks,)), dma((chunks,)), dma((chunks,)), dma((chunks,)), dma((2,))],
        compiler_params=params(56),
        cost_estimate=cost(12),
    )(p, r, d, after)


def strip_kernel(zl_ref, zr_ref, dx_ref, fl_ref, fr_ref, dlo_ref, dhi_ref, xp_ref, xn_ref, pd_ref, gw_ref, in_s, out_s, t_s):
    ny = zl_ref.shape[1]
    row = lax.broadcasted_iota(jnp.int32, (24, ny), 0)
    col = lax.broadcasted_iota(jnp.int32, (24, ny), 1)
    inside = (row < 18) | (row > 21)
    gap = jnp.zeros((2, ny), F32)

    def xy(v):
        near = pltpu.roll(v, 1, 0) + pltpu.roll(v, 23, 0)
        near = near + jnp.where(col == 0, 0.0, pltpu.roll(v, 1, 1))
        return near + jnp.where(col == ny - 1, 0.0, pltpu.roll(v, ny - 1, 1))

    outer_gains = []
    for side, (own_ref, far_ref) in enumerate(((zl_ref, fl_ref), (zr_ref, fr_ref))):
        for q in range(10):
            in_s[q, 0:16, :] = own_ref[q * 16 : q * 16 + 16, :]
            in_s[q, 16:19, :] = own_ref[192 + q * 3 : 192 + q * 3 + 3, :]
            in_s[q, 19:21, :] = gap
            in_s[q, 21:24, :] = own_ref[160 + q * 3 : 160 + q * 3 + 3, :]
            out_s[q, 0:16, :] = far_ref[q * 16 : q * 16 + 16, :]
            out_s[q, 16:19, :] = far_ref[192 + q * 3 : 192 + q * 3 + 3, :]
            out_s[q, 19:21, :] = gap
            out_s[q, 21:24, :] = far_ref[160 + q * 3 : 160 + q * 3 + 3, :]

        def pi(k):
            return in_s[k]

        def po(k):
            return out_s[k]

        gi = [jnp.where(inside, gain(in_s[7 + k]), 0.0) for k in range(3)]
        go = [jnp.where(inside, gain(out_s[7 + k]), 0.0) for k in range(3)]
        outer_gains.append(go)

        def first(g, r, mine, a, b):
            return jnp.where(inside, g * (r + a + b + xy(mine)) - 0.8 * mine, 0.0)

        e0o2 = first(go[2], out_s[6], po(2), po(3), po(1))
        e0o1 = first(go[1], out_s[5], po(1), po(2), po(0))
        e0o0 = first(go[0], out_s[4], po(0), po(1), pi(0))
        e0i0 = first(gi[0], in_s[4], pi(0), po(0), pi(1))
        e0i1 = first(gi[1], in_s[5], pi(1), pi(0), pi(2))
        e1o1 = 1.2 * e0o1 + go[1] * (e0o2 + e0o0 + xy(e0o1))
        e1o0 = 1.2 * e0o0 + go[0] * (e0o1 + e0i0 + xy(e0o0))
        e1i0 = 1.2 * e0i0 + gi[0] * (e0o0 + e0i1 + xy(e0i0))
        e2o0 = 0.2 * e1o0 + e0o0 + go[0] * (e1o1 + e1i0 + xy(e1o0))
        d00 = gi[0] * po(0)
        d10 = 1.2 * d00 + gi[0] * (e0o0 + xy(d00))
        d11 = gi[1] * d00
        d20 = 0.2 * d10 + d00 + gi[0] * (e1o0 + d11 + xy(d10))
        d21 = 0.2 * d11 + gi[1] * (d10 + xy(d11))
        d22 = gi[2] * d11
        d30 = 0.2 * d20 + d00 + gi[0] * (e2o0 + d21 + xy(d20))
        d31 = 0.2 * d21 + gi[1] * (d20 + d22 + xy(d21))
        d32 = 0.2 * d22 + gi[2] * (d21 + xy(d22))
        d33 = gain(dx_ref[side]) * d22[0:16]
        for k, v in enumerate((d30[0:16], d31[0:16], d32[0:16], d33)):
            for b in range(ny // 128):
                t_s[b, pl.ds(4 + k if side == 0 else 3 - k, 16, stride=8), :] = v[:, b * 128 : b * 128 + 128]
    for b in range(ny // 128):
        pd_ref[b * 128 : b * 128 + 128, :] = t_s[b].T

    lane = lax.broadcasted_iota(jnp.int32, (24, 128), 1)
    for wall, (d_ref, part, base) in enumerate(((dlo_ref, 0, 384), (dhi_ref, xp_ref.shape[0] - 1, 504))):
        for j in range(4):
            y = j if wall == 0 else 7 - j
            big = j if wall == 0 else ny - 1 - j
            gw_ref[wall, j, 0:16, 0:128] = gain(d_ref[:, y, :])
            gw_ref[wall, j, 16:24, 0:128] = jnp.zeros((8, 128), F32)
            gw_ref[wall, j, 16:17, 0:128] = xn_ref[part, base + y : base + y + 1, :]
            gw_ref[wall, j, 17:18, 0:128] = xn_ref[part, base + 128 + y : base + 129 + y, :]
            gw_ref[wall, j, 22:23, 0:128] = xp_ref[part, base + 128 + y : base + 129 + y, :]
            gw_ref[wall, j, 23:24, 0:128] = xp_ref[part, base + y : base + y + 1, :]
            acc = jnp.zeros((24, 128), F32)
            for k in range(3):
                acc = jnp.where(lane == 127 - k, outer_gains[0][k][:, big : big + 1], acc)
                acc = jnp.where(lane == k, outer_gains[1][k][:, big : big + 1], acc)
            gw_ref[wall, j, :, 128:256] = acc


def strips(zl, zr, dx, far_l, far_r, d, x_prev, x_next):
    nx, ny, nz = d.shape
    last = ny // 8 - 1

    def whole(a):
        return pl.BlockSpec(a.shape, lambda i: (0,) * a.ndim)

    def wall(n, at):
        return pl.BlockSpec((n, 8, nz), lambda i: (0, at, 0))

    return pl.pallas_call(
        strip_kernel,
        grid=(1,),
        in_specs=[whole(a) for a in (zl, zr, dx, far_l, far_r)]
        + [wall(nx, 0), wall(nx, last), whole(x_prev), whole(x_next)],
        out_specs=[pl.BlockSpec((ny, 128), lambda i: (0, 0)), pl.BlockSpec((2, 4, 24, 256), lambda i: (0, 0, 0, 0))],
        out_shape=[sds(ny, 128), sds(2, 4, 24, 256)],
        scratch_shapes=[pltpu.VMEM((10, 24, ny), F32), pltpu.VMEM((10, 24, ny), F32), pltpu.VMEM((ny // 128, 128, 128), F32)],
        compiler_params=params(56),
        cost_estimate=cost(3),
    )(zl, zr, dx, far_l, far_r, d, d, x_prev, x_next)


def join_kernel(o_hbm, pd_ref, xp_ref, xn_ref, xl_ref, xr_ref, e1_ref, d_hbm, out_hbm, o_s, tall_s, add_s, d_ref, i_sem, o_sem, d_sem):
    nx, ny, nz = o_hbm.shape
    chunks = ny // CH

    def rows(c):
        return pl.ds(pl.multiple_of(c * CH, CH), CH)

    def i_copy(c):
        return pltpu.make_async_copy(o_hbm.at[:, rows(c), :], o_s.at[:, rows(c), :], i_sem.at[c])

    def o_copy(c):
        return pltpu.make_async_copy(o_s.at[:, rows(c), :], out_hbm.at[:, rows(c), :], o_sem.at[c])

    d_copies = [pltpu.make_async_copy(d_hbm.at[x], d_ref.at[k], d_sem.at[k]) for k, x in enumerate((2, 3, nx - 3, nx - 4))]
    for copy in d_copies:
        copy.start()
    for c in range(chunks):
        i_copy(c).start()
    for k in range(tall_s.shape[0]):
        tall_s[k, 0:8, :] = jnp.zeros((8, nz), F32)
        tall_s[k, ny + 8 : ny + 16, :] = jnp.zeros((8, nz), F32)

    def yz(k, c, mine):
        start = c * CH + 8
        return tall_s[k, pl.ds(start - 1, CH), :] + tall_s[k, pl.ds(start + 1, CH), :] + span(mine)

    def each(c, side, far, own, stage):
        r = rows(c)
        t = pl.ds(pl.multiple_of(c * CH + 8, 8), CH)
        b = side * 9
        part = c // 2
        low = (c % 2) * CH

        def of(ref, k):
            return ref[part, pl.ds(pl.multiple_of(k * 128 + low, CH), CH), :]

        gm1, gm2, g0, g1 = of(far, 3), of(far, 4), of(own, 3), of(own, 4)
        if stage == 0:
            tall_s[b, t, :] = of(far, 1) + gm1 * of(own, 0)
            tall_s[b + 1, t, :] = of(far, 2)
            tall_s[b + 2, t, :] = g0 * of(far, 0)
            return
        em1, em2, d00 = tall_s[b, t, :], tall_s[b + 1, t, :], tall_s[b + 2, t, :]
        if stage == 1:
            tall_s[b + 3, t, :] = 1.2 * em1 + gm1 * (em2 + of(own, 1) + d00 + yz(b, c, em1))
            tall_s[b + 4, t, :] = 1.2 * em2 + gm2 * (em1 + yz(b + 1, c, em2))
            tall_s[b + 5, t, :] = 1.2 * d00 + g0 * (em1 + yz(b + 2, c, d00))
            tall_s[b + 6, t, :] = g1 * d00
            return
        e1m1, e1m2, d10, d11 = (tall_s[b + k, t, :] for k in (3, 4, 5, 6))
        g2 = gain(d_ref[2 * side, r, :])
        if stage == 2:
            e2m1 = 0.2 * e1m1 + em1 + gm1 * (e1m2 + e1_ref[side, r, :] + d10 + yz(b + 3, c, e1m1))
            d20 = 0.2 * d10 + d00 + g0 * (e1m1 + d11 + yz(b + 5, c, d10))
            d21 = 0.2 * d11 + g1 * (d10 + yz(b + 6, c, d11))
            d22 = g2 * d11
            tall_s[b, t, :] = e2m1
            tall_s[b + 1, t, :] = d20
            tall_s[b + 7, t, :] = d21
            tall_s[b + 8, t, :] = d22
            return
        e2m1, d20, d21, d22 = (tall_s[b + k, t, :] for k in (0, 1, 7, 8))
        g3 = gain(d_ref[2 * side + 1, r, :])
        d30 = 0.2 * d20 + d00 + g0 * (e2m1 + d21 + yz(b + 1, c, d20))
        d31 = 0.2 * d21 + g1 * (d20 + d22 + yz(b + 7, c, d21))
        d32 = 0.2 * d22 + g2 * (d21 + yz(b + 8, c, d22))
        d33 = g3 * d22
        for k, v in enumerate((d30, d31, d32, d33)):
            add_s[k if side == 0 else 7 - k, :, :] = v

    def stage_loop(stage):
        def body(c, carry):
            each(c, 0, xp_ref, xl_ref, stage)
            each(c, 1, xn_ref, xr_ref, stage)
            return carry

        lax.fori_loop(0, chunks, body, 0)

    stage_loop(0)
    stage_loop(1)
    for copy in d_copies:
        copy.wait()
    stage_loop(2)

    lane = lax.broadcasted_iota(jnp.int32, (CH, nz), 1)
    edge = (lane < 4) | (lane > nz - 5)

    def final(c, carry):
        each(c, 0, xp_ref, xl_ref, 3)
        each(c, 1, xn_ref, xr_ref, 3)
        i_copy(c).wait()
        r = rows(c)
        packed = pd_ref[r, :]
        for x in range(nx):
            strip = jnp.where(edge, pltpu.roll(packed, (128 - 4 - 8 * x) % 128, 1), 0.0)
            v = o_s[x, r, :] + strip
            if x < 4:
                v = v + add_s[x]
            if x >= nx - 4:
                v = v + add_s[x - nx + 8]
            o_s[x, r, :] = v
        o_copy(c).start()
        return carry

    lax.fori_loop(0, chunks, final, 0)
    for c in range(chunks):
        o_copy(c).wait()


def join(out, packed, x_prev, x_next, x_left, x_right, e1, d):
    nx, ny, nz = out.shape
    chunks = ny // CH
    return pl.pallas_call(
        join_kernel,
        out_shape=sds(nx, ny, nz),
        in_specs=[HBM] + [VMEM] * 6 + [HBM],
        out_specs=HBM,
        scratch_shapes=[
            pltpu.VMEM((nx, ny, nz), F32),
            pltpu.VMEM((18, ny + 16, nz), F32),
            pltpu.VMEM((8, CH, nz), F32),
            pltpu.VMEM((4, ny, nz), F32),
            pltpu.SemaphoreType.DMA((chunks,)),
            pltpu.SemaphoreType.DMA((chunks,)),
            pltpu.SemaphoreType.DMA((4,)),
        ],
        input_output_aliases={0: 0},
        compiler_params=params(26),
        cost_estimate=cost(9),
    )(out, packed, x_prev, x_next, x_left, x_right, e1, d)


def finish_kernel(lo_ref, w_ref, wp_ref, wn_ref, l_ref, r_ref, gw_ref, out_ref):
    wall = pl.program_id(0)
    lane = lax.broadcasted_iota(jnp.int32, (24, 128), 1)
    half = lax.broadcasted_iota(jnp.int32, (8, 128), 0)
    at = pl.multiple_of(wall * 16, 16)

    def rows(mine, before, after):
        return jnp.concatenate([mine, jnp.where(half < 4, after[0:8], before[8:16])], axis=0)

    def take(ref, base):
        return ref[pl.ds(pl.multiple_of(base + at, 16), 16), :]

    centre = rows(take(w_ref, 0), take(wp_ref, 0), take(wn_ref, 0))
    left = rows(take(l_ref, 0), take(l_ref, 32), take(l_ref, 64))
    right = rows(take(r_ref, 0), take(r_ref, 32), take(r_ref, 64))
    beyond = jnp.where(lane < 3, right, jnp.where(lane > 124, left, 0.0))
    w = jnp.concatenate([centre, beyond], axis=1)
    g = [gw_ref[0, j] for j in range(4)]

    def xz(v):
        return pltpu.roll(v, 1, 0) + pltpu.roll(v, 23, 0) + pltpu.roll(v, 1, 1) + pltpu.roll(v, 255, 1)

    e0 = g[0] * w
    a0 = 1.2 * e0 + g[0] * xz(e0)
    a1 = g[1] * e0
    b0 = 0.2 * a0 + e0 + g[0] * (a1 + xz(a0))
    b1 = 0.2 * a1 + g[1] * (a0 + xz(a1))
    b2 = g[2] * a1
    c0 = 0.2 * b0 + e0 + g[0] * (b1 + xz(b0))
    c1 = 0.2 * b1 + g[1] * (b0 + b2 + xz(b1))
    c2 = 0.2 * b2 + g[2] * (b1 + xz(b2))
    c3 = g[3] * b2
    for x in range(16):
        out_ref[x] = lo_ref[x]

    def put(ys):
        for y, v in zip(ys, (c0, c1, c2, c3)):
            out_ref[:, y, :] = out_ref[:, y, :] + v[0:16, 0:128]

    @pl.when(wall == 0)
    def _():
        put((0, 1, 2, 3))

    @pl.when(wall == 1)
    def _():
        put((7, 6, 5, 4))


def finish(out, w, w_prev, w_next, left, right, gw):
    nx, ny, nz = out.shape
    last = ny // 8 - 1
    block = pl.BlockSpec((nx, 8, nz), lambda i: (0, i * last, 0))

    def whole(a):
        return pl.BlockSpec(a.shape, lambda i: (0,) * a.ndim)

    return pl.pallas_call(
        finish_kernel,
        grid=(2,),
        out_shape=sds(nx, ny, nz),
        in_specs=[block] + [whole(a) for a in (w, w_prev, w_next, left, right)] + [pl.BlockSpec((1, 4, 24, 256), lambda i: (i, 0, 0, 0))],
        out_specs=block,
        input_output_aliases={0: 0},
        compiler_params=params(8),
        cost_estimate=cost(2),
    )(out, w, w_prev, w_next, left, right, gw)


def trio_kernel(a_ref, b_ref, c_ref, after_ref, out_ref):
    for k, ref in enumerate((a_ref, b_ref, c_ref)):
        out_ref[k * 32 : k * 32 + 32, :] = ref[...]


def trio_of(a, b, c, after):
    return pl.pallas_call(trio_kernel, out_shape=sds(96, 128), in_specs=[VMEM] * 3 + [HBM], out_specs=VMEM, compiler_params=params(4), cost_estimate=cost(1))(a, b, c, after)


def shift(block, axis, distance):
    size = lax.axis_size(axis)
    return lax.ppermute(block, axis, [((i - distance) % size, i) for i in range(size)])


def local(right_side, pressure, diagonal, corrections, wall_cells, owners):
    n_dev = lax.axis_size("gx") * lax.axis_size("gz")
    slots = pack(corrections, wall_cells, owners, n_dev)
    got = lax.all_to_all(slots.reshape(n_dev, 8, 128), AXES, split_axis=0, concat_axis=0, tiled=True).reshape(n_dev * 8, 128)

    zl, zr, dx, x_left, x_right = edges(pressure, right_side, diagonal, slots)
    x_prev = shift(x_right, "gx", 1)
    x_next = shift(x_left, "gx", -1)
    out, e1, token = main_part(pressure, right_side, diagonal, x_left)
    zl, zr = relay(zl, zr, x_prev, x_next, token)
    far_l = shift(zr, "gz", 1)
    far_r = shift(zl, "gz", -1)
    w = wall_sums(got, token)
    w_prev = shift(w, "gx", 1)
    w_next = shift(w, "gx", -1)
    packed, gw = strips(zl, zr, dx, far_l, far_r, diagonal, x_prev, x_next)
    trio = trio_of(w, w_prev, w_next, packed)
    left = shift(trio, "gz", 1)
    right = shift(trio, "gz", -1)
    out = join(out, packed, x_prev, x_next, x_left, x_right, e1, diagonal)
    return finish(out, w, w_prev, w_next, left, right, gw)


def solution(mesh):
    in_specs = (
        P("gx", None, "gz"),
        P("gx", None, "gz"),
        P("gx", None, "gz"),
        P(AXES, None),
        P(AXES, None),
        P(AXES, None),
    )
    return jax.shard_map(local, mesh=mesh, in_specs=in_specs, out_specs=P("gx", None, "gz"), check_vma=False)
```

```python
import jax
import jax.numpy as jnp
from jax import lax
from jax.experimental import pallas as pl
from jax.experimental.pallas import tpu as pltpu
from jax.sharding import PartitionSpec as P

F32 = jnp.float32
BF16 = jnp.bfloat16
AXES = ("gx", "gz")
VMEM = pl.BlockSpec(memory_space=pltpu.VMEM)
HBM = pl.BlockSpec(memory_space=pl.ANY)
MIB = 2**20


def sds(*shape):
    return jax.ShapeDtypeStruct(shape, F32)


def params(mib):
    return pltpu.CompilerParams(vmem_limit_bytes=mib * MIB)


def cost(us):
    return pl.CostEstimate(flops=0, transcendentals=0, bytes_accessed=us * 3_000_000)


def gain(diag):
    return 0.8 / (6.0 + diag)


def pack_kernel(corr_ref, cell_ref, own_ref, out_ref):
    blocks = corr_ref.shape[0]
    rows = out_ref.shape[0]
    own_row = own_ref[...].astype(F32)
    row = lax.broadcasted_iota(jnp.int32, (blocks, blocks), 0)
    col = lax.broadcasted_iota(jnp.int32, (blocks, blocks), 1)
    own = jnp.sum(jnp.where(row == col, own_row, 0.0), axis=1, keepdims=True)
    same = jnp.where((own == own_row) & (row < col), 1.0, 0.0)
    slot = own_row * 8.0 + jnp.sum(same, axis=0, keepdims=True)
    index = lax.broadcasted_iota(jnp.int32, (rows, blocks), 0).astype(F32)
    put_v = jnp.where(index == slot, 1.0, 0.0).astype(BF16)
    put_c = jnp.where(index == slot + 4.0, 1.0, 0.0).astype(BF16)
    vals = corr_ref[...]
    high = vals.astype(BF16)
    rest = vals - high.astype(F32)
    mid = rest.astype(BF16)
    low = (rest - mid.astype(F32)).astype(BF16)
    cells = cell_ref[...]
    major = (cells // 128).astype(F32).astype(BF16)
    minor = (cells % 128).astype(F32).astype(BF16)

    def put(place, what):
        return jnp.dot(place, what, preferred_element_type=F32)

    sent = put(put_v, high) + put(put_v, mid) + put(put_v, low)
    out_ref[...] = sent + (put(put_c, major) * 128.0 + put(put_c, minor))


def pack(corrections, wall_cells, owners, n_dev):
    return pl.pallas_call(
        pack_kernel,
        out_shape=sds(n_dev * 8, corrections.shape[1]),
        in_specs=[VMEM] * 3,
        out_specs=VMEM,
        compiler_params=params(56),
        cost_estimate=cost(3),
    )(corrections, wall_cells, owners.reshape(1, -1))


def wall_kernel(got_ref, w_ref, high_s, low_s, major_s, minor_s):
    rows = got_ref.shape[0]
    got = got_ref[...]
    high = got.astype(BF16).astype(F32)
    high_s[...] = high
    low_s[...] = got - high
    major = jnp.floor(got * (1.0 / 128.0))
    major_s[...] = major
    minor_s[...] = got - major * 128.0
    many = 8
    row_id = lax.broadcasted_iota(jnp.int32, (32, 128), 0).astype(F32)
    col_id = lax.broadcasted_iota(jnp.int32, (128, 128), 0).astype(F32)

    def spread(ref, at, n):
        return jnp.broadcast_to(ref[pl.ds(at, 1), :], (n, 128))

    def step(i, total):
        lefts, rights = [], []
        for k in range(many):
            at = i * (2 * many) + (k // 4) * 8 + k % 4
            hit = spread(major_s, at + 4, 32) == row_id
            top = jnp.where(hit, spread(high_s, at, 32), 0.0).astype(BF16)
            end = jnp.where(hit, spread(low_s, at, 32), 0.0).astype(BF16)
            lefts.append(jnp.concatenate([top, end], axis=0))
            hot = spread(minor_s, at + 4, 128) == col_id
            rights.append(jnp.where(hot, 1.0, 0.0).astype(BF16))
        left = jnp.concatenate(lefts, axis=1)
        right = jnp.concatenate(rights, axis=1)
        return total + lax.dot_general(
            left, right, (((1,), (1,)), ((), ())), preferred_element_type=F32
        )

    total = lax.fori_loop(0, rows // (2 * many), step, jnp.zeros((64, 128), F32), unroll=8)
    w_ref[...] = total[:32] + total[32:]


def wall_sums(got):
    scratch = [pltpu.VMEM(got.shape, F32)] * 4
    return pl.pallas_call(
        wall_kernel,
        out_shape=sds(32, 128),
        in_specs=[VMEM],
        out_specs=VMEM,
        scratch_shapes=scratch,
        compiler_params=params(16),
        cost_estimate=cost(7),
    )(got)


def edge_kernel(p_ref, pu_ref, pd_ref, r_ref, d_ref, after_ref, zl_ref, zr_ref, dx_ref, xl_ref, xr_ref, pk_s, t_s):
    i = pl.program_id(0)
    lane = lax.broadcasted_iota(jnp.int32, (32, 128), 1)
    small = 640
    base = 0
    for which, (ref, depth) in enumerate(((p_ref, 4), (r_ref, 3), (d_ref, 3))):
        for sub in range(4):
            acc = None
            for x in range(16):
                moved = pltpu.roll(ref[x, sub * 32 : sub * 32 + 32, :], (x * 8 + 4) % 128, 1)
                acc = moved if acc is None else jnp.where(lane // 8 == x, moved, acc)
            pk_s[which, sub * 32 : sub * 32 + 32, :] = acc
        t_s[which] = pk_s[which].T
        for k in range(4):
            left = t_s[which, pl.ds(4 + k, 16, stride=8), :]
            right = t_s[which, pl.ds(3 - k, 16, stride=8), :]
            if k < depth:
                q = base + k
                zl_ref[q * 16 : q * 16 + 16, :] = left
                zr_ref[q * 16 : q * 16 + 16, :] = right
                for side, v in enumerate((left, right)):
                    at = small + side * 32 + q * 3
                    xl_ref[0, at : at + 3, :] = v[0:3]
                    xr_ref[0, at : at + 3, :] = v[13:16]
            elif which == 2:
                dx_ref[0] = left
                dx_ref[1] = right
        base += depth

    row = lax.broadcasted_iota(jnp.int32, (128, 128), 0)
    col = lax.broadcasted_iota(jnp.int32, (128, 128), 1)
    first = jnp.where(i > 0, 1.0, 0.0)
    last = jnp.where(i < pl.num_programs(0) - 1, 1.0, 0.0)

    def level0(x, nbrs):
        mine = p_ref[x]
        up = jnp.where(row == 0, pu_ref[x, 7:8, :] * first, pltpu.roll(mine, 1, 0))
        down = jnp.where(row == 127, pd_ref[x, 0:1, :] * last, pltpu.roll(mine, 127, 0))
        near = up + down
        near = near + jnp.where(col == 0, 0.0, pltpu.roll(mine, 1, 1))
        near = near + jnp.where(col == 127, 0.0, pltpu.roll(mine, 127, 1))
        for n in nbrs:
            near = near + p_ref[n]
        g = gain(d_ref[x])
        return g * (r_ref[x] + near) - 0.8 * mine, g

    for ref, edge, inner, third in ((xl_ref, 0, 1, 2), (xr_ref, 15, 14, 13)):
        ref[0, 0:128, :] = p_ref[edge]
        e, g = level0(edge, (inner,))
        ref[0, 128:256, :] = e
        ref[0, 384:512, :] = g
        e, g = level0(inner, (edge, third))
        ref[0, 256:384, :] = e
        ref[0, 512:640, :] = g
        for side in range(2):
            ref[0, small + side * 32 + 30 : small + side * 32 + 32, :] = jnp.zeros((2, 128), F32)


def edges(p, r, d, after):
    nx, ny, nz = p.shape
    whole = pl.BlockSpec((nx, 128, 128), lambda i: (0, i, 0))
    above = pl.BlockSpec((nx, 8, 128), lambda i: (0, jnp.maximum(16 * i - 1, 0), 0))
    under = pl.BlockSpec((nx, 8, 128), lambda i: (0, jnp.minimum(16 * i + 16, ny // 8 - 1), 0))
    strip = pl.BlockSpec((160, 128), lambda i: (0, i))
    return pl.pallas_call(
        edge_kernel,
        grid=(ny // 128,),
        in_specs=[whole, above, under, whole, whole, HBM],
        out_specs=[
            strip,
            strip,
            pl.BlockSpec((2, nx, 128), lambda i: (0, 0, i)),
            pl.BlockSpec((1, 704, nz), lambda i: (i, 0, 0)),
            pl.BlockSpec((1, 704, nz), lambda i: (i, 0, 0)),
        ],
        out_shape=[sds(224, ny), sds(224, ny), sds(2, nx, ny), sds(ny // 128, 704, nz), sds(ny // 128, 704, nz)],
        scratch_shapes=[pltpu.VMEM((3, 128, 128), F32), pltpu.VMEM((3, 128, 128), F32)],
        compiler_params=params(56),
        cost_estimate=cost(9),
    )(p, p, p, r, d, after)


def relay_kernel(zl_in, zr_in, xp_ref, xn_ref, after_ref, zl_ref, zr_ref, sem):
    copies = []
    for side, z in enumerate((zl_ref, zr_ref)):
        for k, x in enumerate((xp_ref, xn_ref)):
            for b in range(x.shape[0]):
                at = 640 + side * 32
                lanes = z.at[160 + 32 * k : 192 + 32 * k, b * 128 : b * 128 + 128]
                copies.append(pltpu.make_async_copy(x.at[b, at : at + 32, :], lanes, sem.at[len(copies)]))
    for c in copies:
        c.start()
    for c in copies:
        c.wait()


def relay(zl, zr, x_prev, x_next, after):
    return pl.pallas_call(
        relay_kernel,
        out_shape=[sds(*zl.shape), sds(*zr.shape)],
        in_specs=[HBM] * 5,
        out_specs=[HBM] * 2,
        scratch_shapes=[pltpu.SemaphoreType.DMA((4 * x_prev.shape[0],))],
        input_output_aliases={0: 0, 1: 1},
        compiler_params=params(4),
        cost_estimate=cost(1),
    )(zl, zr, x_prev, x_next, after)


CH = 64


def span(mine):
    col = lax.broadcasted_iota(jnp.int32, mine.shape, 1)
    near = jnp.where(col == 0, 0.0, pltpu.roll(mine, 1, 1))
    return near + jnp.where(col == mine.shape[1] - 1, 0.0, pltpu.roll(mine, mine.shape[1] - 1, 1))


def beside(n):
    a = lax.broadcasted_iota(jnp.int32, (2 * n, n), 0) % n
    b = lax.broadcasted_iota(jnp.int32, (2 * n, n), 1)
    return jnp.where((a == b + 1) | (a == b - 1), 1.0, 0.0).astype(BF16)


def spans(v, place):
    high = v.astype(BF16)
    low = (v - high.astype(F32)).astype(BF16)
    return jnp.dot(jnp.concatenate([high, low], axis=1), place, preferred_element_type=F32)


def main_kernel(p_hbm, r_hbm, d_hbm, after_ref, out_hbm, e1_hbm, gr_ref, p_s, g_s, e0_s, e1_s, e2_s, p_sem, r_sem, d_sem, o_sem, e_sem):
    nx, ny, nz = p_hbm.shape
    chunks = ny // CH

    def rows(c):
        return pl.ds(pl.multiple_of(c * CH, CH), CH)

    def held(c):
        return pl.ds(pl.multiple_of(8 + c * CH, 8), CH)

    def p_copy(c):
        return pltpu.make_async_copy(p_hbm.at[:, rows(c), :], p_s.at[:, held(c), :], p_sem.at[c])

    def r_copy(c):
        return pltpu.make_async_copy(r_hbm.at[:, rows(c), :], e0_s.at[:, held(c), :], r_sem.at[c])

    def d_copy(c):
        return pltpu.make_async_copy(d_hbm.at[:, rows(c), :], g_s.at[:, rows(c), :], d_sem.at[c])

    def o_copy(c):
        return pltpu.make_async_copy(p_s.at[:, held(c), :], out_hbm.at[:, rows(c), :], o_sem.at[c])

    p_copy(0).start()
    for c in range(chunks):
        r_copy(c).start()
        d_copy(c).start()
        if c + 1 < chunks:
            p_copy(c + 1).start()
    for ref in (p_s, e0_s, e1_s, e2_s):
        for x in range(nx):
            ref[x, 0:8, :] = jnp.zeros((8, nz), F32)
            ref[x, ny + 8 : ny + 16, :] = jnp.zeros((8, nz), F32)
    nothing = jnp.zeros((CH, nz), F32)
    place = beside(nz)
    half = nx // 2

    def sweep(src, c, update):
        start = c * CH + 8
        here = pl.ds(pl.multiple_of(start, 8), CH)
        even = jnp.concatenate([src[2 * q, here, :] for q in range(half)], axis=0)
        sums = spans(even, place).reshape(half, CH, nz)
        before, mine = nothing, src[0, here, :]
        for x in range(nx):
            after = src[x + 1, here, :] if x + 1 < nx else nothing
            near = before + after + src[x, pl.ds(start - 1, CH), :] + src[x, pl.ds(start + 1, CH), :]
            update(x, mine, near + (sums[x // 2] if x % 2 == 0 else span(mine)), here)
            before, mine = mine, after

    def level0(c):
        here_g = rows(c)

        def update(x, mine, near, here):
            g = gain(g_s[x, here_g, :])
            g_s[x, here_g, :] = g
            e0_s[x, here, :] = g * (e0_s[x, here, :] + near) - 0.8 * mine

        sweep(p_s, c, update)

    def level1(c):
        here_g = rows(c)

        def update(x, mine, near, here):
            e1_s[x, here, :] = 1.2 * mine + g_s[x, here_g, :] * near

        sweep(e0_s, c, update)

    def level2(c):
        here_g = rows(c)

        def update(x, mine, near, here):
            e2_s[x, here, :] = 0.2 * mine + e0_s[x, here, :] + g_s[x, here_g, :] * near

        sweep(e1_s, c, update)

    def level3(c):
        here_g = rows(c)

        def update(x, mine, near, here):
            e3 = 0.2 * mine + e0_s[x, here, :] + g_s[x, here_g, :] * near
            p_s[x, here, :] = p_s[x, here, :] + e3

        sweep(e2_s, c, update)
        o_copy(c).start()

    p_copy(0).wait()

    def turn(c, carry):
        @pl.when(c < chunks)
        def _():
            @pl.when(c + 1 < chunks)
            def _():
                p_copy(c + 1).wait()

            r_copy(c).wait()
            d_copy(c).wait()
            level0(c)

        for k, level in ((1, level1), (2, level2), (3, level3)):

            @pl.when((c >= k) & (c - k < chunks))
            def _(k=k, level=level):
                level(c - k)

        return carry

    lax.fori_loop(0, chunks + 3, turn, 0)
    sent = [pltpu.make_async_copy(e1_s.at[x, pl.ds(8, ny), :], e1_hbm.at[k], e_sem.at[k]) for k, x in enumerate((0, nx - 1))]
    for s in sent:
        s.start()
    for x in range(nx):
        gr_ref[0, x] = g_s[x, 0:8, :]
        gr_ref[1, x] = g_s[x, ny - 8 : ny, :]
    for s in sent:
        s.wait()
    for c in range(chunks):
        o_copy(c).wait()


def main_part(p, r, d, after):
    nx, ny, nz = p.shape
    chunks = ny // CH
    tall = pltpu.VMEM((nx, ny + 16, nz), F32)
    dma = pltpu.SemaphoreType.DMA
    return pl.pallas_call(
        main_kernel,
        out_shape=[sds(nx, ny, nz), sds(2, ny, nz), sds(2, nx, 8, nz)],
        in_specs=[HBM] * 4,
        out_specs=[HBM, HBM, VMEM],
        scratch_shapes=[tall, pltpu.VMEM((nx, ny, nz), F32), tall, tall, tall, dma((chunks,)), dma((chunks,)), dma((chunks,)), dma((chunks,)), dma((2,))],
        compiler_params=params(56),
        cost_estimate=cost(12),
    )(p, r, d, after)


def strip_kernel(zl_ref, zr_ref, dx_ref, fl_ref, fr_ref, p1_lo, p2_lo, p1_hi, p2_hi, n1_lo, n2_lo, n1_hi, n2_hi, pd_ref, gw_ref, in_s, out_s, t_s):
    ny = zl_ref.shape[1]
    row = lax.broadcasted_iota(jnp.int32, (24, ny), 0)
    col = lax.broadcasted_iota(jnp.int32, (24, ny), 1)
    inside = (row < 18) | (row > 21)
    gap = jnp.zeros((2, ny), F32)

    def xy(v):
        near = pltpu.roll(v, 1, 0) + pltpu.roll(v, 23, 0)
        near = near + jnp.where(col == 0, 0.0, pltpu.roll(v, 1, 1))
        return near + jnp.where(col == ny - 1, 0.0, pltpu.roll(v, ny - 1, 1))

    outer_gains = []
    for side, (own_ref, far_ref) in enumerate(((zl_ref, fl_ref), (zr_ref, fr_ref))):
        for q in range(10):
            in_s[q, 0:16, :] = own_ref[q * 16 : q * 16 + 16, :]
            in_s[q, 16:19, :] = own_ref[192 + q * 3 : 192 + q * 3 + 3, :]
            in_s[q, 19:21, :] = gap
            in_s[q, 21:24, :] = own_ref[160 + q * 3 : 160 + q * 3 + 3, :]
            out_s[q, 0:16, :] = far_ref[q * 16 : q * 16 + 16, :]
            out_s[q, 16:19, :] = far_ref[192 + q * 3 : 192 + q * 3 + 3, :]
            out_s[q, 19:21, :] = gap
            out_s[q, 21:24, :] = far_ref[160 + q * 3 : 160 + q * 3 + 3, :]

        def pi(k):
            return in_s[k]

        def po(k):
            return out_s[k]

        gi = [jnp.where(inside, gain(in_s[7 + k]), 0.0) for k in range(3)]
        go = [jnp.where(inside, gain(out_s[7 + k]), 0.0) for k in range(3)]
        outer_gains.append(go)

        def first(g, r, mine, a, b):
            return jnp.where(inside, g * (r + a + b + xy(mine)) - 0.8 * mine, 0.0)

        e0o2 = first(go[2], out_s[6], po(2), po(3), po(1))
        e0o1 = first(go[1], out_s[5], po(1), po(2), po(0))
        e0o0 = first(go[0], out_s[4], po(0), po(1), pi(0))
        e0i0 = first(gi[0], in_s[4], pi(0), po(0), pi(1))
        e0i1 = first(gi[1], in_s[5], pi(1), pi(0), pi(2))
        e1o1 = 1.2 * e0o1 + go[1] * (e0o2 + e0o0 + xy(e0o1))
        e1o0 = 1.2 * e0o0 + go[0] * (e0o1 + e0i0 + xy(e0o0))
        e1i0 = 1.2 * e0i0 + gi[0] * (e0o0 + e0i1 + xy(e0i0))
        e2o0 = 0.2 * e1o0 + e0o0 + go[0] * (e1o1 + e1i0 + xy(e1o0))
        d00 = gi[0] * po(0)
        d10 = 1.2 * d00 + gi[0] * (e0o0 + xy(d00))
        d11 = gi[1] * d00
        d20 = 0.2 * d10 + d00 + gi[0] * (e1o0 + d11 + xy(d10))
        d21 = 0.2 * d11 + gi[1] * (d10 + xy(d11))
        d22 = gi[2] * d11
        d30 = 0.2 * d20 + d00 + gi[0] * (e2o0 + d21 + xy(d20))
        d31 = 0.2 * d21 + gi[1] * (d20 + d22 + xy(d21))
        d32 = 0.2 * d22 + gi[2] * (d21 + xy(d22))
        d33 = gain(dx_ref[side]) * d22[0:16]
        for k, v in enumerate((d30[0:16], d31[0:16], d32[0:16], d33)):
            for b in range(ny // 128):
                t_s[b, pl.ds(4 + k if side == 0 else 3 - k, 16, stride=8), :] = v[:, b * 128 : b * 128 + 128]
    for b in range(ny // 128):
        pd_ref[b * 128 : b * 128 + 128, :] = t_s[b].T

    lane = lax.broadcasted_iota(jnp.int32, (24, 128), 1)
    for wall, (p1_ref, p2_ref, n1_ref, n2_ref) in enumerate(((p1_lo, p2_lo, n1_lo, n2_lo), (p1_hi, p2_hi, n1_hi, n2_hi))):
        for j in range(4):
            y = j if wall == 0 else 7 - j
            big = j if wall == 0 else ny - 1 - j
            gw_ref[wall, j, :, 0:128] = jnp.zeros((24, 128), F32)
            gw_ref[wall, j, 16:17, 0:128] = n1_ref[0, y : y + 1, :]
            gw_ref[wall, j, 17:18, 0:128] = n2_ref[0, y : y + 1, :]
            gw_ref[wall, j, 22:23, 0:128] = p2_ref[0, y : y + 1, :]
            gw_ref[wall, j, 23:24, 0:128] = p1_ref[0, y : y + 1, :]
            acc = jnp.zeros((24, 128), F32)
            for k in range(3):
                acc = jnp.where(lane == 127 - k, outer_gains[0][k][:, big : big + 1], acc)
                acc = jnp.where(lane == k, outer_gains[1][k][:, big : big + 1], acc)
            gw_ref[wall, j, :, 128:256] = acc


def strips(zl, zr, dx, far_l, far_r, x_prev, x_next):
    ny, nz = zl.shape[1], x_prev.shape[2]

    def whole(a):
        return pl.BlockSpec(a.shape, lambda i: (0,) * a.ndim)

    far = x_prev.shape[0] - 1

    def halo(part, at):
        return pl.BlockSpec((1, 8, nz), lambda i: (part, at, 0))

    return pl.pallas_call(
        strip_kernel,
        grid=(1,),
        in_specs=[whole(a) for a in (zl, zr, dx, far_l, far_r)]
        + [halo(0, 48), halo(0, 64), halo(far, 63), halo(far, 79)] * 2,
        out_specs=[pl.BlockSpec((ny, 128), lambda i: (0, 0)), pl.BlockSpec((2, 4, 24, 256), lambda i: (0, 0, 0, 0))],
        out_shape=[sds(ny, 128), sds(2, 4, 24, 256)],
        scratch_shapes=[pltpu.VMEM((10, 24, ny), F32), pltpu.VMEM((10, 24, ny), F32), pltpu.VMEM((ny // 128, 128, 128), F32)],
        compiler_params=params(20),
        cost_estimate=cost(3),
    )(zl, zr, dx, far_l, far_r, *[x_prev] * 4, *[x_next] * 4)


def join_kernel(o_hbm, pd_ref, xp_ref, xn_ref, xl_ref, xr_ref, e1_ref, d_hbm, out_hbm, rim_ref, o_s, tall_s, add_s, d_ref, i_sem, o_sem, d_sem):
    nx, ny, nz = o_hbm.shape
    chunks = ny // CH

    def rows(c):
        return pl.ds(pl.multiple_of(c * CH, CH), CH)

    def i_copy(c):
        return pltpu.make_async_copy(o_hbm.at[:, rows(c), :], o_s.at[:, rows(c), :], i_sem.at[c])

    def o_copy(c):
        return pltpu.make_async_copy(o_s.at[:, rows(c), :], out_hbm.at[:, rows(c), :], o_sem.at[c])

    d_copies = [pltpu.make_async_copy(d_hbm.at[x], d_ref.at[k], d_sem.at[k]) for k, x in enumerate((2, 3, nx - 3, nx - 4))]
    for copy in d_copies:
        copy.start()
    for c in range(chunks):
        i_copy(c).start()
    for k in range(tall_s.shape[0]):
        tall_s[k, 0:8, :] = jnp.zeros((8, nz), F32)
        tall_s[k, ny + 8 : ny + 16, :] = jnp.zeros((8, nz), F32)

    def yz(k, c, mine):
        start = c * CH + 8
        return tall_s[k, pl.ds(start - 1, CH), :] + tall_s[k, pl.ds(start + 1, CH), :] + span(mine)

    def each(c, side, far, own, stage):
        r = rows(c)
        t = pl.ds(pl.multiple_of(c * CH + 8, 8), CH)
        b = side * 9
        part = c // 2
        low = (c % 2) * CH

        def of(ref, k):
            return ref[part, pl.ds(pl.multiple_of(k * 128 + low, CH), CH), :]

        gm1, gm2, g0, g1 = of(far, 3), of(far, 4), of(own, 3), of(own, 4)
        if stage == 0:
            tall_s[b, t, :] = of(far, 1) + gm1 * of(own, 0)
            tall_s[b + 1, t, :] = of(far, 2)
            tall_s[b + 2, t, :] = g0 * of(far, 0)
            return
        em1, em2, d00 = tall_s[b, t, :], tall_s[b + 1, t, :], tall_s[b + 2, t, :]
        if stage == 1:
            tall_s[b + 3, t, :] = 1.2 * em1 + gm1 * (em2 + of(own, 1) + d00 + yz(b, c, em1))
            tall_s[b + 4, t, :] = 1.2 * em2 + gm2 * (em1 + yz(b + 1, c, em2))
            tall_s[b + 5, t, :] = 1.2 * d00 + g0 * (em1 + yz(b + 2, c, d00))
            tall_s[b + 6, t, :] = g1 * d00
            return
        e1m1, e1m2, d10, d11 = (tall_s[b + k, t, :] for k in (3, 4, 5, 6))
        g2 = gain(d_ref[2 * side, r, :])
        if stage == 2:
            e2m1 = 0.2 * e1m1 + em1 + gm1 * (e1m2 + e1_ref[side, r, :] + d10 + yz(b + 3, c, e1m1))
            d20 = 0.2 * d10 + d00 + g0 * (e1m1 + d11 + yz(b + 5, c, d10))
            d21 = 0.2 * d11 + g1 * (d10 + yz(b + 6, c, d11))
            d22 = g2 * d11
            tall_s[b, t, :] = e2m1
            tall_s[b + 1, t, :] = d20
            tall_s[b + 7, t, :] = d21
            tall_s[b + 8, t, :] = d22
            return
        e2m1, d20, d21, d22 = (tall_s[b + k, t, :] for k in (0, 1, 7, 8))
        g3 = gain(d_ref[2 * side + 1, r, :])
        d30 = 0.2 * d20 + d00 + g0 * (e2m1 + d21 + yz(b + 1, c, d20))
        d31 = 0.2 * d21 + g1 * (d20 + d22 + yz(b + 7, c, d21))
        d32 = 0.2 * d22 + g2 * (d21 + yz(b + 8, c, d22))
        d33 = g3 * d22
        for k, v in enumerate((d30, d31, d32, d33)):
            add_s[k if side == 0 else 7 - k, :, :] = v

    def stage_loop(stage):
        def body(c, carry):
            each(c, 0, xp_ref, xl_ref, stage)
            each(c, 1, xn_ref, xr_ref, stage)
            return carry

        lax.fori_loop(0, chunks, body, 0)

    stage_loop(0)
    stage_loop(1)
    for copy in d_copies:
        copy.wait()
    stage_loop(2)

    lane = lax.broadcasted_iota(jnp.int32, (CH, nz), 1)
    edge = (lane < 4) | (lane > nz - 5)

    def final(c, carry):
        each(c, 0, xp_ref, xl_ref, 3)
        each(c, 1, xn_ref, xr_ref, 3)
        i_copy(c).wait()
        r = rows(c)
        packed = pd_ref[r, :]
        for x in range(nx):
            strip = jnp.where(edge, pltpu.roll(packed, (128 - 4 - 8 * x) % 128, 1), 0.0)
            v = o_s[x, r, :] + strip
            if x < 4:
                v = v + add_s[x]
            if x >= nx - 4:
                v = v + add_s[x - nx + 8]
            o_s[x, r, :] = v
        o_copy(c).start()
        return carry

    lax.fori_loop(0, chunks, final, 0)
    for x in range(nx):
        rim_ref[0, x] = o_s[x, 0:8, :]
        rim_ref[1, x] = o_s[x, ny - 8 : ny, :]
    for c in range(chunks):
        o_copy(c).wait()


def join(out, packed, x_prev, x_next, x_left, x_right, e1, d):
    nx, ny, nz = out.shape
    chunks = ny // CH
    return pl.pallas_call(
        join_kernel,
        out_shape=[sds(nx, ny, nz), sds(2, nx, 8, nz)],
        in_specs=[HBM] + [VMEM] * 6 + [HBM],
        out_specs=[HBM, VMEM],
        scratch_shapes=[
            pltpu.VMEM((nx, ny, nz), F32),
            pltpu.VMEM((18, ny + 16, nz), F32),
            pltpu.VMEM((8, CH, nz), F32),
            pltpu.VMEM((4, ny, nz), F32),
            pltpu.SemaphoreType.DMA((chunks,)),
            pltpu.SemaphoreType.DMA((chunks,)),
            pltpu.SemaphoreType.DMA((4,)),
        ],
        input_output_aliases={0: 0},
        compiler_params=params(26),
        cost_estimate=cost(9),
    )(out, packed, x_prev, x_next, x_left, x_right, e1, d)


def finish_kernel(o_hbm, rim_ref, w_ref, wp_ref, wn_ref, l_ref, r_ref, gw_ref, gr_ref, out_hbm, new_s, sem):
    lane = lax.broadcasted_iota(jnp.int32, (24, 128), 1)
    half = lax.broadcasted_iota(jnp.int32, (8, 128), 0)
    ny = out_hbm.shape[1]
    copies = []
    for wall in range(2):
        at = wall * 16

        def rows(mine, before, after):
            return jnp.concatenate([mine, jnp.where(half < 4, after[0:8], before[8:16])], axis=0)

        def take(ref, base):
            return ref[base + at : base + at + 16, :]

        centre = rows(take(w_ref, 0), take(wp_ref, 0), take(wn_ref, 0))
        left = rows(take(l_ref, 0), take(l_ref, 32), take(l_ref, 64))
        right = rows(take(r_ref, 0), take(r_ref, 32), take(r_ref, 64))
        beyond = jnp.where(lane < 3, right, jnp.where(lane > 124, left, 0.0))
        w = jnp.concatenate([centre, beyond], axis=1)
        g = []
        for j in range(4):
            mine = gr_ref[wall, :, j if wall == 0 else 7 - j, :]
            halo = gw_ref[wall, j]
            g.append(jnp.concatenate([jnp.concatenate([mine, halo[16:24, 0:128]], axis=0), halo[:, 128:256]], axis=1))

        def xz(v):
            return pltpu.roll(v, 1, 0) + pltpu.roll(v, 23, 0) + pltpu.roll(v, 1, 1) + pltpu.roll(v, 255, 1)

        e0 = g[0] * w
        a0 = 1.2 * e0 + g[0] * xz(e0)
        a1 = g[1] * e0
        b0 = 0.2 * a0 + e0 + g[0] * (a1 + xz(a0))
        b1 = 0.2 * a1 + g[1] * (a0 + xz(a1))
        b2 = g[2] * a1
        c0 = 0.2 * b0 + e0 + g[0] * (b1 + xz(b0))
        c1 = 0.2 * b1 + g[1] * (b0 + b2 + xz(b1))
        c2 = 0.2 * b2 + g[2] * (b1 + xz(b2))
        c3 = g[3] * b2
        new_s[wall] = rim_ref[wall]
        for j, v in enumerate((c0, c1, c2, c3)):
            y = j if wall == 0 else 7 - j
            new_s[wall, :, y, :] = new_s[wall, :, y, :] + v[0:16, 0:128]
        first = 0 if wall == 0 else ny - 8
        copies.append(pltpu.make_async_copy(new_s.at[wall], out_hbm.at[:, first : first + 8, :], sem.at[wall]))
        copies[wall].start()
    for copy in copies:
        copy.wait()


def finish(out, edge_rows, w, w_prev, w_next, left, right, gw, g_rows):
    nx, ny, nz = out.shape
    return pl.pallas_call(
        finish_kernel,
        out_shape=sds(nx, ny, nz),
        in_specs=[HBM] + [VMEM] * 8,
        out_specs=HBM,
        scratch_shapes=[pltpu.VMEM((2, nx, 8, nz), F32), pltpu.SemaphoreType.DMA((2,))],
        input_output_aliases={0: 0},
        compiler_params=params(8),
        cost_estimate=cost(2),
    )(out, edge_rows, w, w_prev, w_next, left, right, gw, g_rows)


def trio_kernel(a_ref, b_ref, c_ref, after_ref, out_ref):
    for k, ref in enumerate((a_ref, b_ref, c_ref)):
        out_ref[k * 32 : k * 32 + 32, :] = ref[...]


def trio_of(a, b, c, after):
    return pl.pallas_call(trio_kernel, out_shape=sds(96, 128), in_specs=[VMEM] * 3 + [HBM], out_specs=VMEM, compiler_params=params(4), cost_estimate=cost(1))(a, b, c, after)


def shift(block, axis, distance):
    size = lax.axis_size(axis)
    return lax.ppermute(block, axis, [((i - distance) % size, i) for i in range(size)])


def local(right_side, pressure, diagonal, corrections, wall_cells, owners):
    n_dev = lax.axis_size("gx") * lax.axis_size("gz")
    slots = pack(corrections, wall_cells, owners, n_dev)
    got = lax.all_to_all(slots.reshape(n_dev, 8, 128), AXES, split_axis=0, concat_axis=0, tiled=True).reshape(n_dev * 8, 128)

    zl, zr, dx, x_left, x_right = edges(pressure, right_side, diagonal, slots)
    x_prev = shift(x_right, "gx", 1)
    x_next = shift(x_left, "gx", -1)
    out, e1, g_rows = main_part(pressure, right_side, diagonal, x_left)
    zl, zr = relay(zl, zr, x_prev, x_next, g_rows)
    far_l = shift(zr, "gz", 1)
    far_r = shift(zl, "gz", -1)
    w = wall_sums(got)
    w_prev = shift(w, "gx", 1)
    w_next = shift(w, "gx", -1)
    packed, gw = strips(zl, zr, dx, far_l, far_r, x_prev, x_next)
    trio = trio_of(w, w_prev, w_next, packed)
    left = shift(trio, "gz", 1)
    right = shift(trio, "gz", -1)
    out, edge_rows = join(out, packed, x_prev, x_next, x_left, x_right, e1, diagonal)
    return finish(out, edge_rows, w, w_prev, w_next, left, right, gw, g_rows)


def solution(mesh):
    in_specs = (
        P("gx", None, "gz"),
        P("gx", None, "gz"),
        P("gx", None, "gz"),
        P(AXES, None),
        P(AXES, None),
        P(AXES, None),
    )
    return jax.shard_map(local, mesh=mesh, in_specs=in_specs, out_specs=P("gx", None, "gz"), check_vma=False)
```

```python
import jax
import jax.numpy as jnp
from jax import lax
from jax.experimental import pallas as pl
from jax.experimental.pallas import tpu as pltpu
from jax.sharding import PartitionSpec as P

F32 = jnp.float32
BF16 = jnp.bfloat16
AXES = ("gx", "gz")
VMEM = pl.BlockSpec(memory_space=pltpu.VMEM)
HBM = pl.BlockSpec(memory_space=pl.ANY)
MIB = 2**20


def sds(*shape):
    return jax.ShapeDtypeStruct(shape, F32)


def params(mib):
    return pltpu.CompilerParams(vmem_limit_bytes=mib * MIB)


def cost(us):
    return pl.CostEstimate(flops=0, transcendentals=0, bytes_accessed=us * 3_000_000)


def gain(diag):
    return 0.8 / (6.0 + diag)


def pack_kernel(corr_ref, cell_ref, own_ref, out_ref):
    blocks = corr_ref.shape[0]
    rows = out_ref.shape[0]
    own_row = own_ref[...].astype(F32)
    row = lax.broadcasted_iota(jnp.int32, (blocks, blocks), 0)
    col = lax.broadcasted_iota(jnp.int32, (blocks, blocks), 1)
    own = jnp.sum(jnp.where(row == col, own_row, 0.0), axis=1, keepdims=True)
    same = jnp.where((own == own_row) & (row < col), 1.0, 0.0)
    slot = own_row * 8.0 + jnp.sum(same, axis=0, keepdims=True)
    index = lax.broadcasted_iota(jnp.int32, (rows, blocks), 0).astype(F32)
    put_v = jnp.where(index == slot, 1.0, 0.0).astype(BF16)
    put_c = jnp.where(index == slot + 4.0, 1.0, 0.0).astype(BF16)
    vals = corr_ref[...]
    high = vals.astype(BF16)
    rest = vals - high.astype(F32)
    mid = rest.astype(BF16)
    low = (rest - mid.astype(F32)).astype(BF16)
    cells = cell_ref[...]
    major = (cells // 128).astype(F32).astype(BF16)
    minor = (cells % 128).astype(F32).astype(BF16)

    def put(place, what):
        return jnp.dot(place, what, preferred_element_type=F32)

    sent = put(put_v, high) + put(put_v, mid) + put(put_v, low)
    out_ref[...] = sent + (put(put_c, major) * 128.0 + put(put_c, minor))


def pack(corrections, wall_cells, owners, n_dev):
    return pl.pallas_call(
        pack_kernel,
        out_shape=sds(n_dev * 8, corrections.shape[1]),
        in_specs=[VMEM] * 3,
        out_specs=VMEM,
        compiler_params=params(56),
        cost_estimate=cost(3),
    )(corrections, wall_cells, owners.reshape(1, -1))


def wall_kernel(got_ref, w_ref, high_s, low_s, major_s, minor_s):
    rows = got_ref.shape[0]
    got = got_ref[...]
    high = got.astype(BF16).astype(F32)
    high_s[...] = high
    low_s[...] = got - high
    major = jnp.floor(got * (1.0 / 128.0))
    major_s[...] = major
    minor_s[...] = got - major * 128.0
    many = 16
    row_id = lax.broadcasted_iota(jnp.int32, (32, 128), 0).astype(F32)
    col_id = lax.broadcasted_iota(jnp.int32, (128, 128), 0).astype(F32)

    def spread(ref, at, n):
        return jnp.broadcast_to(ref[pl.ds(at, 1), :], (n, 128))

    def step(i, total):
        lefts, rights = [], []
        for k in range(many):
            at = i * (2 * many) + (k // 4) * 8 + k % 4
            hit = spread(major_s, at + 4, 32) == row_id
            top = jnp.where(hit, spread(high_s, at, 32), 0.0).astype(BF16)
            end = jnp.where(hit, spread(low_s, at, 32), 0.0).astype(BF16)
            lefts.append(jnp.concatenate([top, end], axis=0))
            hot = spread(minor_s, at + 4, 128) == col_id
            rights.append(jnp.where(hot, 1.0, 0.0).astype(BF16))
        left = jnp.concatenate(lefts, axis=1)
        right = jnp.concatenate(rights, axis=1)
        return total + lax.dot_general(
            left, right, (((1,), (1,)), ((), ())), preferred_element_type=F32
        )

    total = lax.fori_loop(0, rows // (2 * many), step, jnp.zeros((64, 128), F32), unroll=8)
    w_ref[...] = total[:32] + total[32:]


def wall_sums(got):
    scratch = [pltpu.VMEM(got.shape, F32)] * 4
    return pl.pallas_call(
        wall_kernel,
        out_shape=sds(32, 128),
        in_specs=[VMEM],
        out_specs=VMEM,
        scratch_shapes=scratch,
        compiler_params=params(16),
        cost_estimate=cost(7),
    )(got)


def edge_kernel(p_ref, pu_ref, pd_ref, r_ref, d_ref, after_ref, zl_ref, zr_ref, dx_ref, xl_ref, xr_ref, pk_s, t_s):
    i = pl.program_id(0)
    lane = lax.broadcasted_iota(jnp.int32, (32, 128), 1)
    small = 640
    base = 0
    for which, (ref, depth) in enumerate(((p_ref, 4), (r_ref, 3), (d_ref, 3))):
        for sub in range(4):
            acc = None
            for x in range(16):
                moved = pltpu.roll(ref[x, sub * 32 : sub * 32 + 32, :], (x * 8 + 4) % 128, 1)
                acc = moved if acc is None else jnp.where(lane // 8 == x, moved, acc)
            pk_s[which, sub * 32 : sub * 32 + 32, :] = acc
        t_s[which] = pk_s[which].T
        for k in range(4):
            left = t_s[which, pl.ds(4 + k, 16, stride=8), :]
            right = t_s[which, pl.ds(3 - k, 16, stride=8), :]
            if k < depth:
                q = base + k
                zl_ref[q * 16 : q * 16 + 16, :] = left
                zr_ref[q * 16 : q * 16 + 16, :] = right
                for side, v in enumerate((left, right)):
                    at = small + side * 32 + q * 3
                    xl_ref[0, at : at + 3, :] = v[0:3]
                    xr_ref[0, at : at + 3, :] = v[13:16]
            elif which == 2:
                dx_ref[0] = left
                dx_ref[1] = right
        base += depth

    row = lax.broadcasted_iota(jnp.int32, (128, 128), 0)
    col = lax.broadcasted_iota(jnp.int32, (128, 128), 1)
    first = jnp.where(i > 0, 1.0, 0.0)
    last = jnp.where(i < pl.num_programs(0) - 1, 1.0, 0.0)

    def level0(x, nbrs):
        mine = p_ref[x]
        up = jnp.where(row == 0, pu_ref[x, 7:8, :] * first, pltpu.roll(mine, 1, 0))
        down = jnp.where(row == 127, pd_ref[x, 0:1, :] * last, pltpu.roll(mine, 127, 0))
        near = up + down
        near = near + jnp.where(col == 0, 0.0, pltpu.roll(mine, 1, 1))
        near = near + jnp.where(col == 127, 0.0, pltpu.roll(mine, 127, 1))
        for n in nbrs:
            near = near + p_ref[n]
        g = gain(d_ref[x])
        return g * (r_ref[x] + near) - 0.8 * mine, g

    for ref, edge, inner, third in ((xl_ref, 0, 1, 2), (xr_ref, 15, 14, 13)):
        ref[0, 0:128, :] = p_ref[edge]
        e, g = level0(edge, (inner,))
        ref[0, 128:256, :] = e
        ref[0, 384:512, :] = g
        e, g = level0(inner, (edge, third))
        ref[0, 256:384, :] = e
        ref[0, 512:640, :] = g
        for side in range(2):
            ref[0, small + side * 32 + 30 : small + side * 32 + 32, :] = jnp.zeros((2, 128), F32)


def edges(p, r, d, after):
    nx, ny, nz = p.shape
    whole = pl.BlockSpec((nx, 128, 128), lambda i: (0, i, 0))
    above = pl.BlockSpec((nx, 8, 128), lambda i: (0, jnp.maximum(16 * i - 1, 0), 0))
    under = pl.BlockSpec((nx, 8, 128), lambda i: (0, jnp.minimum(16 * i + 16, ny // 8 - 1), 0))
    strip = pl.BlockSpec((160, 128), lambda i: (0, i))
    return pl.pallas_call(
        edge_kernel,
        grid=(ny // 128,),
        in_specs=[whole, above, under, whole, whole, HBM],
        out_specs=[
            strip,
            strip,
            pl.BlockSpec((2, nx, 128), lambda i: (0, 0, i)),
            pl.BlockSpec((1, 704, nz), lambda i: (i, 0, 0)),
            pl.BlockSpec((1, 704, nz), lambda i: (i, 0, 0)),
        ],
        out_shape=[sds(224, ny), sds(224, ny), sds(2, nx, ny), sds(ny // 128, 704, nz), sds(ny // 128, 704, nz)],
        scratch_shapes=[pltpu.VMEM((3, 128, 128), F32), pltpu.VMEM((3, 128, 128), F32)],
        compiler_params=params(56),
        cost_estimate=cost(9),
    )(p, p, p, r, d, after)


def relay_kernel(zl_in, zr_in, xp_ref, xn_ref, zl_ref, zr_ref, sem):
    copies = []
    for side, z in enumerate((zl_ref, zr_ref)):
        for k, x in enumerate((xp_ref, xn_ref)):
            for b in range(x.shape[0]):
                at = 640 + side * 32
                lanes = z.at[160 + 32 * k : 192 + 32 * k, b * 128 : b * 128 + 128]
                copies.append(pltpu.make_async_copy(x.at[b, at : at + 32, :], lanes, sem.at[len(copies)]))
    for c in copies:
        c.start()
    for c in copies:
        c.wait()


def relay(zl, zr, x_prev, x_next):
    return pl.pallas_call(
        relay_kernel,
        out_shape=[sds(*zl.shape), sds(*zr.shape)],
        in_specs=[HBM] * 4,
        out_specs=[HBM] * 2,
        scratch_shapes=[pltpu.SemaphoreType.DMA((4 * x_prev.shape[0],))],
        input_output_aliases={0: 0, 1: 1},
        compiler_params=params(4),
        cost_estimate=cost(1),
    )(zl, zr, x_prev, x_next)


CH = 64


def span(mine):
    col = lax.broadcasted_iota(jnp.int32, mine.shape, 1)
    near = jnp.where(col == 0, 0.0, pltpu.roll(mine, 1, 1))
    return near + jnp.where(col == mine.shape[1] - 1, 0.0, pltpu.roll(mine, mine.shape[1] - 1, 1))


def beside(n):
    a = lax.broadcasted_iota(jnp.int32, (2 * n, n), 0) % n
    b = lax.broadcasted_iota(jnp.int32, (2 * n, n), 1)
    return jnp.where((a == b + 1) | (a == b - 1), 1.0, 0.0).astype(BF16)


def spans(v, place):
    high = v.astype(BF16)
    low = (v - high.astype(F32)).astype(BF16)
    return jnp.dot(jnp.concatenate([high, low], axis=1), place, preferred_element_type=F32)


def main_kernel(p_hbm, r_hbm, d_hbm, after_ref, out_hbm, e1_hbm, gr_ref, p_s, g_s, e0_s, e1_s, e2_s, p_sem, r_sem, d_sem, o_sem, e_sem):
    nx, ny, nz = p_hbm.shape
    chunks = ny // CH

    def rows(c):
        return pl.ds(pl.multiple_of(c * CH, CH), CH)

    def held(c):
        return pl.ds(pl.multiple_of(8 + c * CH, 8), CH)

    def p_copy(c):
        return pltpu.make_async_copy(p_hbm.at[:, rows(c), :], p_s.at[:, held(c), :], p_sem.at[c])

    def r_copy(c):
        return pltpu.make_async_copy(r_hbm.at[:, rows(c), :], e0_s.at[:, held(c), :], r_sem.at[c])

    def d_copy(c):
        return pltpu.make_async_copy(d_hbm.at[:, rows(c), :], g_s.at[:, rows(c), :], d_sem.at[c])

    def o_copy(c):
        return pltpu.make_async_copy(p_s.at[:, held(c), :], out_hbm.at[:, rows(c), :], o_sem.at[c])

    p_copy(0).start()
    for c in range(chunks):
        r_copy(c).start()
        d_copy(c).start()
        if c + 1 < chunks:
            p_copy(c + 1).start()
    for ref in (p_s, e0_s, e1_s, e2_s):
        for x in range(nx):
            ref[x, 0:8, :] = jnp.zeros((8, nz), F32)
            ref[x, ny + 8 : ny + 16, :] = jnp.zeros((8, nz), F32)
    nothing = jnp.zeros((CH, nz), F32)
    place = beside(nz)
    half = nx // 2

    def sweep(src, c, update):
        start = c * CH + 8
        here = pl.ds(pl.multiple_of(start, 8), CH)
        even = jnp.concatenate([src[2 * q, here, :] for q in range(half)], axis=0)
        sums = spans(even, place).reshape(half, CH, nz)
        before, mine = nothing, src[0, here, :]
        for x in range(nx):
            after = src[x + 1, here, :] if x + 1 < nx else nothing
            near = before + after + src[x, pl.ds(start - 1, CH), :] + src[x, pl.ds(start + 1, CH), :]
            update(x, mine, near + (sums[x // 2] if x % 2 == 0 else span(mine)), here)
            before, mine = mine, after

    def level0(c):
        here_g = rows(c)

        def update(x, mine, near, here):
            g = gain(g_s[x, here_g, :])
            g_s[x, here_g, :] = g
            e0_s[x, here, :] = g * (e0_s[x, here, :] + near) - 0.8 * mine

        sweep(p_s, c, update)

    def level1(c):
        here_g = rows(c)

        def update(x, mine, near, here):
            e1_s[x, here, :] = 1.2 * mine + g_s[x, here_g, :] * near

        sweep(e0_s, c, update)

    def level2(c):
        here_g = rows(c)

        def update(x, mine, near, here):
            e2_s[x, here, :] = 0.2 * mine + e0_s[x, here, :] + g_s[x, here_g, :] * near

        sweep(e1_s, c, update)

    def level3(c):
        here_g = rows(c)

        def update(x, mine, near, here):
            e3 = 0.2 * mine + e0_s[x, here, :] + g_s[x, here_g, :] * near
            p_s[x, here, :] = p_s[x, here, :] + e3

        sweep(e2_s, c, update)
        o_copy(c).start()

    p_copy(0).wait()

    def turn(c, carry):
        @pl.when(c < chunks)
        def _():
            @pl.when(c + 1 < chunks)
            def _():
                p_copy(c + 1).wait()

            r_copy(c).wait()
            d_copy(c).wait()
            level0(c)

        for k, level in ((1, level1), (2, level2), (3, level3)):

            @pl.when((c >= k) & (c - k < chunks))
            def _(k=k, level=level):
                level(c - k)

        return carry

    lax.fori_loop(0, chunks + 3, turn, 0)
    sent = [pltpu.make_async_copy(e1_s.at[x, pl.ds(8, ny), :], e1_hbm.at[k], e_sem.at[k]) for k, x in enumerate((0, nx - 1))]
    for s in sent:
        s.start()
    for x in range(nx):
        gr_ref[0, x] = g_s[x, 0:8, :]
        gr_ref[1, x] = g_s[x, ny - 8 : ny, :]
    for s in sent:
        s.wait()
    for c in range(chunks):
        o_copy(c).wait()


def main_part(p, r, d, after):
    nx, ny, nz = p.shape
    chunks = ny // CH
    tall = pltpu.VMEM((nx, ny + 16, nz), F32)
    dma = pltpu.SemaphoreType.DMA
    return pl.pallas_call(
        main_kernel,
        out_shape=[sds(nx, ny, nz), sds(2, ny, nz), sds(2, nx, 8, nz)],
        in_specs=[HBM] * 4,
        out_specs=[HBM, HBM, VMEM],
        scratch_shapes=[tall, pltpu.VMEM((nx, ny, nz), F32), tall, tall, tall, dma((chunks,)), dma((chunks,)), dma((chunks,)), dma((chunks,)), dma((2,))],
        compiler_params=params(56),
        cost_estimate=cost(12),
    )(p, r, d, after)


def strip_kernel(zl_ref, zr_ref, dx_ref, fl_ref, fr_ref, p1_lo, p2_lo, p1_hi, p2_hi, n1_lo, n2_lo, n1_hi, n2_hi, pd_ref, gw_ref, in_s, out_s, t_s):
    ny = zl_ref.shape[1]
    row = lax.broadcasted_iota(jnp.int32, (24, ny), 0)
    col = lax.broadcasted_iota(jnp.int32, (24, ny), 1)
    inside = (row < 18) | (row > 21)
    gap = jnp.zeros((2, ny), F32)

    def xy(v):
        near = pltpu.roll(v, 1, 0) + pltpu.roll(v, 23, 0)
        near = near + jnp.where(col == 0, 0.0, pltpu.roll(v, 1, 1))
        return near + jnp.where(col == ny - 1, 0.0, pltpu.roll(v, ny - 1, 1))

    outer_gains = []
    for side, (own_ref, far_ref) in enumerate(((zl_ref, fl_ref), (zr_ref, fr_ref))):
        for q in range(10):
            in_s[q, 0:16, :] = own_ref[q * 16 : q * 16 + 16, :]
            in_s[q, 16:19, :] = own_ref[192 + q * 3 : 192 + q * 3 + 3, :]
            in_s[q, 19:21, :] = gap
            in_s[q, 21:24, :] = own_ref[160 + q * 3 : 160 + q * 3 + 3, :]
            out_s[q, 0:16, :] = far_ref[q * 16 : q * 16 + 16, :]
            out_s[q, 16:19, :] = far_ref[192 + q * 3 : 192 + q * 3 + 3, :]
            out_s[q, 19:21, :] = gap
            out_s[q, 21:24, :] = far_ref[160 + q * 3 : 160 + q * 3 + 3, :]

        def pi(k):
            return in_s[k]

        def po(k):
            return out_s[k]

        gi = [jnp.where(inside, gain(in_s[7 + k]), 0.0) for k in range(3)]
        go = [jnp.where(inside, gain(out_s[7 + k]), 0.0) for k in range(3)]
        outer_gains.append(go)

        def first(g, r, mine, a, b):
            return jnp.where(inside, g * (r + a + b + xy(mine)) - 0.8 * mine, 0.0)

        e0o2 = first(go[2], out_s[6], po(2), po(3), po(1))
        e0o1 = first(go[1], out_s[5], po(1), po(2), po(0))
        e0o0 = first(go[0], out_s[4], po(0), po(1), pi(0))
        e0i0 = first(gi[0], in_s[4], pi(0), po(0), pi(1))
        e0i1 = first(gi[1], in_s[5], pi(1), pi(0), pi(2))
        e1o1 = 1.2 * e0o1 + go[1] * (e0o2 + e0o0 + xy(e0o1))
        e1o0 = 1.2 * e0o0 + go[0] * (e0o1 + e0i0 + xy(e0o0))
        e1i0 = 1.2 * e0i0 + gi[0] * (e0o0 + e0i1 + xy(e0i0))
        e2o0 = 0.2 * e1o0 + e0o0 + go[0] * (e1o1 + e1i0 + xy(e1o0))
        d00 = gi[0] * po(0)
        d10 = 1.2 * d00 + gi[0] * (e0o0 + xy(d00))
        d11 = gi[1] * d00
        d20 = 0.2 * d10 + d00 + gi[0] * (e1o0 + d11 + xy(d10))
        d21 = 0.2 * d11 + gi[1] * (d10 + xy(d11))
        d22 = gi[2] * d11
        d30 = 0.2 * d20 + d00 + gi[0] * (e2o0 + d21 + xy(d20))
        d31 = 0.2 * d21 + gi[1] * (d20 + d22 + xy(d21))
        d32 = 0.2 * d22 + gi[2] * (d21 + xy(d22))
        d33 = gain(dx_ref[side]) * d22[0:16]
        for k, v in enumerate((d30[0:16], d31[0:16], d32[0:16], d33)):
            for b in range(ny // 128):
                t_s[b, pl.ds(4 + k if side == 0 else 3 - k, 16, stride=8), :] = v[:, b * 128 : b * 128 + 128]
    for b in range(ny // 128):
        pd_ref[b * 128 : b * 128 + 128, :] = t_s[b].T

    lane = lax.broadcasted_iota(jnp.int32, (24, 128), 1)
    for wall, (p1_ref, p2_ref, n1_ref, n2_ref) in enumerate(((p1_lo, p2_lo, n1_lo, n2_lo), (p1_hi, p2_hi, n1_hi, n2_hi))):
        for j in range(4):
            y = j if wall == 0 else 7 - j
            big = j if wall == 0 else ny - 1 - j
            gw_ref[wall, j, :, 0:128] = jnp.zeros((24, 128), F32)
            gw_ref[wall, j, 16:17, 0:128] = n1_ref[0, y : y + 1, :]
            gw_ref[wall, j, 17:18, 0:128] = n2_ref[0, y : y + 1, :]
            gw_ref[wall, j, 22:23, 0:128] = p2_ref[0, y : y + 1, :]
            gw_ref[wall, j, 23:24, 0:128] = p1_ref[0, y : y + 1, :]
            acc = jnp.zeros((24, 128), F32)
            for k in range(3):
                acc = jnp.where(lane == 127 - k, outer_gains[0][k][:, big : big + 1], acc)
                acc = jnp.where(lane == k, outer_gains[1][k][:, big : big + 1], acc)
            gw_ref[wall, j, :, 128:256] = acc


def strips(zl, zr, dx, far_l, far_r, x_prev, x_next):
    ny, nz = zl.shape[1], x_prev.shape[2]

    def whole(a):
        return pl.BlockSpec(a.shape, lambda i: (0,) * a.ndim)

    far = x_prev.shape[0] - 1

    def halo(part, at):
        return pl.BlockSpec((1, 8, nz), lambda i: (part, at, 0))

    return pl.pallas_call(
        strip_kernel,
        grid=(1,),
        in_specs=[whole(a) for a in (zl, zr, dx, far_l, far_r)]
        + [halo(0, 48), halo(0, 64), halo(far, 63), halo(far, 79)] * 2,
        out_specs=[pl.BlockSpec((ny, 128), lambda i: (0, 0)), pl.BlockSpec((2, 4, 24, 256), lambda i: (0, 0, 0, 0))],
        out_shape=[sds(ny, 128), sds(2, 4, 24, 256)],
        scratch_shapes=[pltpu.VMEM((10, 24, ny), F32), pltpu.VMEM((10, 24, ny), F32), pltpu.VMEM((ny // 128, 128, 128), F32)],
        compiler_params=params(20),
        cost_estimate=cost(3),
    )(zl, zr, dx, far_l, far_r, *[x_prev] * 4, *[x_next] * 4)


def join_kernel(o_hbm, pd_ref, xp_ref, xn_ref, xl_ref, xr_ref, e1_ref, d_hbm, out_hbm, rim_ref, o_s, tall_s, add_s, d_ref, i_sem, o_sem, d_sem):
    nx, ny, nz = o_hbm.shape
    chunks = ny // CH

    def rows(c):
        return pl.ds(pl.multiple_of(c * CH, CH), CH)

    def i_copy(c):
        return pltpu.make_async_copy(o_hbm.at[:, rows(c), :], o_s.at[:, rows(c), :], i_sem.at[c])

    def o_copy(c):
        return pltpu.make_async_copy(o_s.at[:, rows(c), :], out_hbm.at[:, rows(c), :], o_sem.at[c])

    d_copies = [pltpu.make_async_copy(d_hbm.at[x], d_ref.at[k], d_sem.at[k]) for k, x in enumerate((2, 3, nx - 3, nx - 4))]
    for copy in d_copies:
        copy.start()
    for c in range(chunks):
        i_copy(c).start()
    for k in range(tall_s.shape[0]):
        tall_s[k, 0:8, :] = jnp.zeros((8, nz), F32)
        tall_s[k, ny + 8 : ny + 16, :] = jnp.zeros((8, nz), F32)

    def yz(k, c, mine):
        start = c * CH + 8
        return tall_s[k, pl.ds(start - 1, CH), :] + tall_s[k, pl.ds(start + 1, CH), :] + span(mine)

    def each(c, side, far, own, stage):
        r = rows(c)
        t = pl.ds(pl.multiple_of(c * CH + 8, 8), CH)
        b = side * 9
        part = c // 2
        low = (c % 2) * CH

        def of(ref, k):
            return ref[part, pl.ds(pl.multiple_of(k * 128 + low, CH), CH), :]

        gm1, gm2, g0, g1 = of(far, 3), of(far, 4), of(own, 3), of(own, 4)
        if stage == 0:
            tall_s[b, t, :] = of(far, 1) + gm1 * of(own, 0)
            tall_s[b + 1, t, :] = of(far, 2)
            tall_s[b + 2, t, :] = g0 * of(far, 0)
            return
        em1, em2, d00 = tall_s[b, t, :], tall_s[b + 1, t, :], tall_s[b + 2, t, :]
        if stage == 1:
            tall_s[b + 3, t, :] = 1.2 * em1 + gm1 * (em2 + of(own, 1) + d00 + yz(b, c, em1))
            tall_s[b + 4, t, :] = 1.2 * em2 + gm2 * (em1 + yz(b + 1, c, em2))
            tall_s[b + 5, t, :] = 1.2 * d00 + g0 * (em1 + yz(b + 2, c, d00))
            tall_s[b + 6, t, :] = g1 * d00
            return
        e1m1, e1m2, d10, d11 = (tall_s[b + k, t, :] for k in (3, 4, 5, 6))
        g2 = gain(d_ref[2 * side, r, :])
        if stage == 2:
            e2m1 = 0.2 * e1m1 + em1 + gm1 * (e1m2 + e1_ref[side, r, :] + d10 + yz(b + 3, c, e1m1))
            d20 = 0.2 * d10 + d00 + g0 * (e1m1 + d11 + yz(b + 5, c, d10))
            d21 = 0.2 * d11 + g1 * (d10 + yz(b + 6, c, d11))
            d22 = g2 * d11
            tall_s[b, t, :] = e2m1
            tall_s[b + 1, t, :] = d20
            tall_s[b + 7, t, :] = d21
            tall_s[b + 8, t, :] = d22
            return
        e2m1, d20, d21, d22 = (tall_s[b + k, t, :] for k in (0, 1, 7, 8))
        g3 = gain(d_ref[2 * side + 1, r, :])
        d30 = 0.2 * d20 + d00 + g0 * (e2m1 + d21 + yz(b + 1, c, d20))
        d31 = 0.2 * d21 + g1 * (d20 + d22 + yz(b + 7, c, d21))
        d32 = 0.2 * d22 + g2 * (d21 + yz(b + 8, c, d22))
        d33 = g3 * d22
        for k, v in enumerate((d30, d31, d32, d33)):
            add_s[k if side == 0 else 7 - k, :, :] = v

    def stage_loop(stage):
        def body(c, carry):
            each(c, 0, xp_ref, xl_ref, stage)
            each(c, 1, xn_ref, xr_ref, stage)
            return carry

        lax.fori_loop(0, chunks, body, 0)

    stage_loop(0)
    stage_loop(1)
    for copy in d_copies:
        copy.wait()
    stage_loop(2)

    lane = lax.broadcasted_iota(jnp.int32, (CH, nz), 1)
    edge = (lane < 4) | (lane > nz - 5)

    def final(c, carry):
        each(c, 0, xp_ref, xl_ref, 3)
        each(c, 1, xn_ref, xr_ref, 3)
        i_copy(c).wait()
        r = rows(c)
        packed = pd_ref[r, :]
        for x in range(nx):
            strip = jnp.where(edge, pltpu.roll(packed, (128 - 4 - 8 * x) % 128, 1), 0.0)
            v = o_s[x, r, :] + strip
            if x < 4:
                v = v + add_s[x]
            if x >= nx - 4:
                v = v + add_s[x - nx + 8]
            o_s[x, r, :] = v
        o_copy(c).start()
        return carry

    lax.fori_loop(0, chunks, final, 0)
    for x in range(nx):
        rim_ref[0, x] = o_s[x, 0:8, :]
        rim_ref[1, x] = o_s[x, ny - 8 : ny, :]
    for c in range(chunks):
        o_copy(c).wait()


def join(out, packed, x_prev, x_next, x_left, x_right, e1, d):
    nx, ny, nz = out.shape
    chunks = ny // CH
    return pl.pallas_call(
        join_kernel,
        out_shape=[sds(nx, ny, nz), sds(2, nx, 8, nz)],
        in_specs=[HBM] + [VMEM] * 6 + [HBM],
        out_specs=[HBM, VMEM],
        scratch_shapes=[
            pltpu.VMEM((nx, ny, nz), F32),
            pltpu.VMEM((18, ny + 16, nz), F32),
            pltpu.VMEM((8, CH, nz), F32),
            pltpu.VMEM((4, ny, nz), F32),
            pltpu.SemaphoreType.DMA((chunks,)),
            pltpu.SemaphoreType.DMA((chunks,)),
            pltpu.SemaphoreType.DMA((4,)),
        ],
        input_output_aliases={0: 0},
        compiler_params=params(26),
        cost_estimate=cost(9),
    )(out, packed, x_prev, x_next, x_left, x_right, e1, d)


def finish_kernel(o_hbm, rim_ref, w_ref, wp_ref, wn_ref, l_ref, r_ref, gw_ref, gr_ref, out_hbm, new_s, sem):
    lane = lax.broadcasted_iota(jnp.int32, (24, 128), 1)
    half = lax.broadcasted_iota(jnp.int32, (8, 128), 0)
    ny = out_hbm.shape[1]
    copies = []
    for wall in range(2):
        at = wall * 16

        def rows(mine, before, after):
            return jnp.concatenate([mine, jnp.where(half < 4, after[0:8], before[8:16])], axis=0)

        def take(ref, base):
            return ref[base + at : base + at + 16, :]

        centre = rows(take(w_ref, 0), take(wp_ref, 0), take(wn_ref, 0))
        left = rows(take(l_ref, 0), take(l_ref, 32), take(l_ref, 64))
        right = rows(take(r_ref, 0), take(r_ref, 32), take(r_ref, 64))
        beyond = jnp.where(lane < 3, right, jnp.where(lane > 124, left, 0.0))
        w = jnp.concatenate([centre, beyond], axis=1)
        g = []
        for j in range(4):
            mine = gr_ref[wall, :, j if wall == 0 else 7 - j, :]
            halo = gw_ref[wall, j]
            g.append(jnp.concatenate([jnp.concatenate([mine, halo[16:24, 0:128]], axis=0), halo[:, 128:256]], axis=1))

        def xz(v):
            return pltpu.roll(v, 1, 0) + pltpu.roll(v, 23, 0) + pltpu.roll(v, 1, 1) + pltpu.roll(v, 255, 1)

        e0 = g[0] * w
        a0 = 1.2 * e0 + g[0] * xz(e0)
        a1 = g[1] * e0
        b0 = 0.2 * a0 + e0 + g[0] * (a1 + xz(a0))
        b1 = 0.2 * a1 + g[1] * (a0 + xz(a1))
        b2 = g[2] * a1
        c0 = 0.2 * b0 + e0 + g[0] * (b1 + xz(b0))
        c1 = 0.2 * b1 + g[1] * (b0 + b2 + xz(b1))
        c2 = 0.2 * b2 + g[2] * (b1 + xz(b2))
        c3 = g[3] * b2
        new_s[wall] = rim_ref[wall]
        for j, v in enumerate((c0, c1, c2, c3)):
            y = j if wall == 0 else 7 - j
            new_s[wall, :, y, :] = new_s[wall, :, y, :] + v[0:16, 0:128]
        first = 0 if wall == 0 else ny - 8
        copies.append(pltpu.make_async_copy(new_s.at[wall], out_hbm.at[:, first : first + 8, :], sem.at[wall]))
        copies[wall].start()
    for copy in copies:
        copy.wait()


def finish(out, edge_rows, w, w_prev, w_next, left, right, gw, g_rows):
    nx, ny, nz = out.shape
    return pl.pallas_call(
        finish_kernel,
        out_shape=sds(nx, ny, nz),
        in_specs=[HBM] + [VMEM] * 8,
        out_specs=HBM,
        scratch_shapes=[pltpu.VMEM((2, nx, 8, nz), F32), pltpu.SemaphoreType.DMA((2,))],
        input_output_aliases={0: 0},
        compiler_params=params(8),
        cost_estimate=cost(2),
    )(out, edge_rows, w, w_prev, w_next, left, right, gw, g_rows)


def trio_kernel(a_ref, b_ref, c_ref, out_ref):
    for k, ref in enumerate((a_ref, b_ref, c_ref)):
        out_ref[k * 32 : k * 32 + 32, :] = ref[...]


def trio_of(a, b, c):
    return pl.pallas_call(trio_kernel, out_shape=sds(96, 128), in_specs=[VMEM] * 3, out_specs=VMEM, compiler_params=params(4), cost_estimate=cost(1))(a, b, c)


def shift(block, axis, distance):
    size = lax.axis_size(axis)
    return lax.ppermute(block, axis, [((i - distance) % size, i) for i in range(size)])


def local(right_side, pressure, diagonal, corrections, wall_cells, owners):
    n_dev = lax.axis_size("gx") * lax.axis_size("gz")
    slots = pack(corrections, wall_cells, owners, n_dev)
    got = lax.all_to_all(slots.reshape(n_dev, 8, 128), AXES, split_axis=0, concat_axis=0, tiled=True).reshape(n_dev * 8, 128)

    zl, zr, dx, x_left, x_right = edges(pressure, right_side, diagonal, slots)
    x_prev = shift(x_right, "gx", 1)
    x_next = shift(x_left, "gx", -1)
    out, e1, g_rows = main_part(pressure, right_side, diagonal, x_left)
    x_prev, x_next, e1 = lax.optimization_barrier((x_prev, x_next, e1))
    zl, zr = relay(zl, zr, x_prev, x_next)
    far_l = shift(zr, "gz", 1)
    far_r = shift(zl, "gz", -1)
    w = wall_sums(got)
    w_prev = shift(w, "gx", 1)
    w_next = shift(w, "gx", -1)
    packed, gw = strips(zl, zr, dx, far_l, far_r, x_prev, x_next)
    w_prev, w_next, packed = lax.optimization_barrier((w_prev, w_next, packed))
    trio = trio_of(w, w_prev, w_next)
    left = shift(trio, "gz", 1)
    right = shift(trio, "gz", -1)
    out, edge_rows = join(out, packed, x_prev, x_next, x_left, x_right, e1, diagonal)
    return finish(out, edge_rows, w, w_prev, w_next, left, right, gw, g_rows)


def solution(mesh):
    in_specs = (
        P("gx", None, "gz"),
        P("gx", None, "gz"),
        P("gx", None, "gz"),
        P(AXES, None),
        P(AXES, None),
        P(AXES, None),
    )
    return jax.shard_map(local, mesh=mesh, in_specs=in_specs, out_specs=P("gx", None, "gz"), check_vma=False)
```

```python
import jax
import jax.numpy as jnp
from jax import lax
from jax.experimental import pallas as pl
from jax.experimental.pallas import tpu as pltpu
from jax.sharding import PartitionSpec as P

F32 = jnp.float32
BF16 = jnp.bfloat16
AXES = ("gx", "gz")
VMEM = pl.BlockSpec(memory_space=pltpu.VMEM)
HBM = pl.BlockSpec(memory_space=pl.ANY)
MIB = 2**20


def sds(*shape):
    return jax.ShapeDtypeStruct(shape, F32)


def params(mib):
    return pltpu.CompilerParams(vmem_limit_bytes=mib * MIB)


def cost(us):
    return pl.CostEstimate(flops=0, transcendentals=0, bytes_accessed=us * 3_000_000)


def gain(diag):
    return 0.8 / (6.0 + diag)


def pack_kernel(corr_ref, cell_ref, own_ref, out_ref):
    blocks = corr_ref.shape[0]
    rows = out_ref.shape[0]
    own_row = own_ref[...].astype(F32)
    row = lax.broadcasted_iota(jnp.int32, (blocks, blocks), 0)
    col = lax.broadcasted_iota(jnp.int32, (blocks, blocks), 1)
    own = jnp.sum(jnp.where(row == col, own_row, 0.0), axis=1, keepdims=True)
    same = jnp.where((own == own_row) & (row < col), 1.0, 0.0)
    slot = own_row * 8.0 + jnp.sum(same, axis=0, keepdims=True)
    index = lax.broadcasted_iota(jnp.int32, (rows, blocks), 0).astype(F32)
    put_v = jnp.where(index == slot, 1.0, 0.0).astype(BF16)
    put_c = jnp.where(index == slot + 4.0, 1.0, 0.0).astype(BF16)
    vals = corr_ref[...]
    high = vals.astype(BF16)
    rest = vals - high.astype(F32)
    mid = rest.astype(BF16)
    cells = cell_ref[...]
    major = (cells // 128).astype(F32).astype(BF16)
    minor = (cells % 128).astype(F32).astype(BF16)

    def put(place, first, second):
        return jnp.dot(place, jnp.concatenate([first, second], axis=1), preferred_element_type=F32)

    value = put(put_v, high, mid)
    cell = put(put_c, major, minor)
    out_ref[...] = value[:, 0:128] + value[:, 128:256] + (cell[:, 0:128] * 128.0 + cell[:, 128:256])


def pack(corrections, wall_cells, owners, n_dev):
    return pl.pallas_call(
        pack_kernel,
        out_shape=sds(n_dev * 8, corrections.shape[1]),
        in_specs=[VMEM] * 3,
        out_specs=VMEM,
        compiler_params=params(56),
        cost_estimate=cost(3),
    )(corrections, wall_cells, owners.reshape(1, -1))


def wall_kernel(got_ref, w_ref, high_s, low_s, major_s, minor_s):
    rows = got_ref.shape[0]
    got = got_ref[...]
    high = got.astype(BF16).astype(F32)
    high_s[...] = high
    low_s[...] = got - high
    major = jnp.floor(got * (1.0 / 128.0))
    major_s[...] = major
    minor_s[...] = got - major * 128.0
    many = 16
    row_id = lax.broadcasted_iota(jnp.int32, (32, 128), 0).astype(F32)
    col_id = lax.broadcasted_iota(jnp.int32, (128, 128), 0).astype(F32)

    def spread(ref, at, n):
        return jnp.broadcast_to(ref[pl.ds(at, 1), :], (n, 128))

    def step(i, total):
        lefts, rights = [], []
        for k in range(many):
            at = i * (2 * many) + (k // 4) * 8 + k % 4
            hit = spread(major_s, at + 4, 32) == row_id
            top = jnp.where(hit, spread(high_s, at, 32), 0.0).astype(BF16)
            end = jnp.where(hit, spread(low_s, at, 32), 0.0).astype(BF16)
            lefts.append(jnp.concatenate([top, end], axis=0))
            hot = spread(minor_s, at + 4, 128) == col_id
            rights.append(jnp.where(hot, 1.0, 0.0).astype(BF16))
        left = jnp.concatenate(lefts, axis=1)
        right = jnp.concatenate(rights, axis=1)
        return total + lax.dot_general(
            left, right, (((1,), (1,)), ((), ())), preferred_element_type=F32
        )

    total = lax.fori_loop(0, rows // (2 * many), step, jnp.zeros((64, 128), F32), unroll=8)
    w_ref[...] = total[:32] + total[32:]


def wall_sums(got):
    scratch = [pltpu.VMEM(got.shape, F32)] * 4
    return pl.pallas_call(
        wall_kernel,
        out_shape=sds(32, 128),
        in_specs=[VMEM],
        out_specs=VMEM,
        scratch_shapes=scratch,
        compiler_params=params(16),
        cost_estimate=cost(7),
    )(got)


def edge_kernel(p_ref, pu_ref, pd_ref, r_ref, d_ref, zl_ref, zr_ref, dx_ref, xl_ref, xr_ref, pk_s, t_s):
    i = pl.program_id(0)
    lane = lax.broadcasted_iota(jnp.int32, (32, 128), 1)
    small = 640
    base = 0
    for which, (ref, depth) in enumerate(((p_ref, 4), (r_ref, 3), (d_ref, 3))):
        for sub in range(4):
            acc = None
            for x in range(16):
                moved = pltpu.roll(ref[x, sub * 32 : sub * 32 + 32, :], (x * 8 + 4) % 128, 1)
                acc = moved if acc is None else jnp.where(lane // 8 == x, moved, acc)
            pk_s[which, sub * 32 : sub * 32 + 32, :] = acc
        t_s[which] = pk_s[which].T
        for k in range(4):
            left = t_s[which, pl.ds(4 + k, 16, stride=8), :]
            right = t_s[which, pl.ds(3 - k, 16, stride=8), :]
            if k < depth:
                q = base + k
                zl_ref[q * 16 : q * 16 + 16, :] = left
                zr_ref[q * 16 : q * 16 + 16, :] = right
                for side, v in enumerate((left, right)):
                    at = small + side * 32 + q * 3
                    xl_ref[0, at : at + 3, :] = v[0:3]
                    xr_ref[0, at : at + 3, :] = v[13:16]
            elif which == 2:
                dx_ref[0] = left
                dx_ref[1] = right
        base += depth

    row = lax.broadcasted_iota(jnp.int32, (128, 128), 0)
    col = lax.broadcasted_iota(jnp.int32, (128, 128), 1)
    first = jnp.where(i > 0, 1.0, 0.0)
    last = jnp.where(i < pl.num_programs(0) - 1, 1.0, 0.0)

    def level0(x, nbrs):
        mine = p_ref[x]
        up = jnp.where(row == 0, pu_ref[x, 7:8, :] * first, pltpu.roll(mine, 1, 0))
        down = jnp.where(row == 127, pd_ref[x, 0:1, :] * last, pltpu.roll(mine, 127, 0))
        near = up + down
        near = near + jnp.where(col == 0, 0.0, pltpu.roll(mine, 1, 1))
        near = near + jnp.where(col == 127, 0.0, pltpu.roll(mine, 127, 1))
        for n in nbrs:
            near = near + p_ref[n]
        g = gain(d_ref[x])
        return g * (r_ref[x] + near) - 0.8 * mine, g

    for ref, edge, inner, third in ((xl_ref, 0, 1, 2), (xr_ref, 15, 14, 13)):
        ref[0, 0:128, :] = p_ref[edge]
        e, g = level0(edge, (inner,))
        ref[0, 128:256, :] = e
        ref[0, 384:512, :] = g
        e, g = level0(inner, (edge, third))
        ref[0, 256:384, :] = e
        ref[0, 512:640, :] = g
        for side in range(2):
            ref[0, small + side * 32 + 30 : small + side * 32 + 32, :] = jnp.zeros((2, 128), F32)


def edges(p, r, d):
    nx, ny, nz = p.shape
    whole = pl.BlockSpec((nx, 128, 128), lambda i: (0, i, 0))
    above = pl.BlockSpec((nx, 8, 128), lambda i: (0, jnp.maximum(16 * i - 1, 0), 0))
    under = pl.BlockSpec((nx, 8, 128), lambda i: (0, jnp.minimum(16 * i + 16, ny // 8 - 1), 0))
    strip = pl.BlockSpec((160, 128), lambda i: (0, i))
    return pl.pallas_call(
        edge_kernel,
        grid=(ny // 128,),
        in_specs=[whole, above, under, whole, whole],
        out_specs=[
            strip,
            strip,
            pl.BlockSpec((2, nx, 128), lambda i: (0, 0, i)),
            pl.BlockSpec((1, 704, nz), lambda i: (i, 0, 0)),
            pl.BlockSpec((1, 704, nz), lambda i: (i, 0, 0)),
        ],
        out_shape=[sds(224, ny), sds(224, ny), sds(2, nx, ny), sds(ny // 128, 704, nz), sds(ny // 128, 704, nz)],
        scratch_shapes=[pltpu.VMEM((3, 128, 128), F32), pltpu.VMEM((3, 128, 128), F32)],
        compiler_params=params(56),
        cost_estimate=cost(9),
    )(p, p, p, r, d)


def relay_kernel(zl_in, zr_in, xp_ref, xn_ref, zl_ref, zr_ref, sem):
    copies = []
    for side, z in enumerate((zl_ref, zr_ref)):
        for k, x in enumerate((xp_ref, xn_ref)):
            for b in range(x.shape[0]):
                at = 640 + side * 32
                lanes = z.at[160 + 32 * k : 192 + 32 * k, b * 128 : b * 128 + 128]
                copies.append(pltpu.make_async_copy(x.at[b, at : at + 32, :], lanes, sem.at[len(copies)]))
    for c in copies:
        c.start()
    for c in copies:
        c.wait()


def relay(zl, zr, x_prev, x_next):
    return pl.pallas_call(
        relay_kernel,
        out_shape=[sds(*zl.shape), sds(*zr.shape)],
        in_specs=[HBM] * 4,
        out_specs=[HBM] * 2,
        scratch_shapes=[pltpu.SemaphoreType.DMA((4 * x_prev.shape[0],))],
        input_output_aliases={0: 0, 1: 1},
        compiler_params=params(4),
        cost_estimate=cost(1),
    )(zl, zr, x_prev, x_next)


CH = 64


def span(mine):
    col = lax.broadcasted_iota(jnp.int32, mine.shape, 1)
    near = jnp.where(col == 0, 0.0, pltpu.roll(mine, 1, 1))
    return near + jnp.where(col == mine.shape[1] - 1, 0.0, pltpu.roll(mine, mine.shape[1] - 1, 1))


def beside(n):
    a = lax.broadcasted_iota(jnp.int32, (2 * n, n), 0) % n
    b = lax.broadcasted_iota(jnp.int32, (2 * n, n), 1)
    return jnp.where((a == b + 1) | (a == b - 1), 1.0, 0.0).astype(BF16)


def spans(v, place):
    high = v.astype(BF16)
    low = (v - high.astype(F32)).astype(BF16)
    return jnp.dot(jnp.concatenate([high, low], axis=1), place, preferred_element_type=F32)


def main_kernel(p_hbm, r_hbm, d_hbm, after_ref, out_hbm, e1_hbm, gr_ref, p_s, g_s, e0_s, e1_s, e2_s, p_sem, r_sem, d_sem, o_sem, e_sem):
    nx, ny, nz = p_hbm.shape
    chunks = ny // CH

    def rows(c):
        return pl.ds(pl.multiple_of(c * CH, CH), CH)

    def held(c):
        return pl.ds(pl.multiple_of(8 + c * CH, 8), CH)

    def p_copy(c):
        return pltpu.make_async_copy(p_hbm.at[:, rows(c), :], p_s.at[:, held(c), :], p_sem.at[c])

    def r_copy(c):
        return pltpu.make_async_copy(r_hbm.at[:, rows(c), :], e0_s.at[:, held(c), :], r_sem.at[c])

    def d_copy(c):
        return pltpu.make_async_copy(d_hbm.at[:, rows(c), :], g_s.at[:, rows(c), :], d_sem.at[c])

    def o_copy(c):
        return pltpu.make_async_copy(p_s.at[:, held(c), :], out_hbm.at[:, rows(c), :], o_sem.at[c])

    p_copy(0).start()
    for c in range(chunks):
        r_copy(c).start()
        d_copy(c).start()
        if c + 1 < chunks:
            p_copy(c + 1).start()
    for ref in (p_s, e0_s, e1_s, e2_s):
        for x in range(nx):
            ref[x, 0:8, :] = jnp.zeros((8, nz), F32)
            ref[x, ny + 8 : ny + 16, :] = jnp.zeros((8, nz), F32)
    nothing = jnp.zeros((CH, nz), F32)
    place = beside(nz)

    def sweep(src, c, update):
        start = c * CH + 8
        here = pl.ds(pl.multiple_of(start, 8), CH)
        before, mine = nothing, src[0, here, :]
        for x in range(nx):
            after = src[x + 1, here, :] if x + 1 < nx else nothing
            if x % 2 == 0 and x % 8 == 0:
                four = jnp.concatenate([src[x + 2 * q, here, :] for q in range(4)], axis=0)
                sums = spans(four, place).reshape(4, CH, nz)
            near = before + after + src[x, pl.ds(start - 1, CH), :] + src[x, pl.ds(start + 1, CH), :]
            update(x, mine, near + (sums[x % 8 // 2] if x % 2 == 0 else span(mine)), here)
            before, mine = mine, after

    def level0(c):
        here_g = rows(c)

        def update(x, mine, near, here):
            g = gain(g_s[x, here_g, :])
            g_s[x, here_g, :] = g
            e0_s[x, here, :] = g * (e0_s[x, here, :] + near) - 0.8 * mine

        sweep(p_s, c, update)

    def level1(c):
        here_g = rows(c)

        def update(x, mine, near, here):
            e1_s[x, here, :] = 1.2 * mine + g_s[x, here_g, :] * near

        sweep(e0_s, c, update)

    def level2(c):
        here_g = rows(c)

        def update(x, mine, near, here):
            e2_s[x, here, :] = 0.2 * mine + e0_s[x, here, :] + g_s[x, here_g, :] * near

        sweep(e1_s, c, update)

    def level3(c):
        here_g = rows(c)

        def update(x, mine, near, here):
            e3 = 0.2 * mine + e0_s[x, here, :] + g_s[x, here_g, :] * near
            p_s[x, here, :] = p_s[x, here, :] + e3

        sweep(e2_s, c, update)
        o_copy(c).start()

    p_copy(0).wait()

    def turn(c, carry):
        @pl.when(c < chunks)
        def _():
            @pl.when(c + 1 < chunks)
            def _():
                p_copy(c + 1).wait()

            r_copy(c).wait()
            d_copy(c).wait()
            level0(c)

        for k, level in ((1, level1), (2, level2), (3, level3)):

            @pl.when((c >= k) & (c - k < chunks))
            def _(k=k, level=level):
                level(c - k)

        return carry

    lax.fori_loop(0, chunks + 3, turn, 0)
    sent = [pltpu.make_async_copy(e1_s.at[x, pl.ds(8, ny), :], e1_hbm.at[k], e_sem.at[k]) for k, x in enumerate((0, nx - 1))]
    for s in sent:
        s.start()
    for x in range(nx):
        gr_ref[0, x] = g_s[x, 0:8, :]
        gr_ref[1, x] = g_s[x, ny - 8 : ny, :]
    for s in sent:
        s.wait()
    for c in range(chunks):
        o_copy(c).wait()


def main_part(p, r, d, after):
    nx, ny, nz = p.shape
    chunks = ny // CH
    tall = pltpu.VMEM((nx, ny + 16, nz), F32)
    dma = pltpu.SemaphoreType.DMA
    return pl.pallas_call(
        main_kernel,
        out_shape=[sds(nx, ny, nz), sds(2, ny, nz), sds(2, nx, 8, nz)],
        in_specs=[HBM] * 4,
        out_specs=[HBM, HBM, VMEM],
        scratch_shapes=[tall, pltpu.VMEM((nx, ny, nz), F32), tall, tall, tall, dma((chunks,)), dma((chunks,)), dma((chunks,)), dma((chunks,)), dma((2,))],
        compiler_params=params(56),
        cost_estimate=cost(12),
    )(p, r, d, after)


def strip_kernel(zl_ref, zr_ref, dx_ref, fl_ref, fr_ref, p1_lo, p2_lo, p1_hi, p2_hi, n1_lo, n2_lo, n1_hi, n2_hi, pd_ref, gw_ref, in_s, out_s, t_s):
    ny = zl_ref.shape[1]
    row = lax.broadcasted_iota(jnp.int32, (24, ny), 0)
    col = lax.broadcasted_iota(jnp.int32, (24, ny), 1)
    inside = (row < 18) | (row > 21)
    gap = jnp.zeros((2, ny), F32)

    def xy(v):
        near = pltpu.roll(v, 1, 0) + pltpu.roll(v, 23, 0)
        near = near + jnp.where(col == 0, 0.0, pltpu.roll(v, 1, 1))
        return near + jnp.where(col == ny - 1, 0.0, pltpu.roll(v, ny - 1, 1))

    outer_gains = []
    for side, (own_ref, far_ref) in enumerate(((zl_ref, fl_ref), (zr_ref, fr_ref))):
        for q in range(10):
            in_s[q, 0:16, :] = own_ref[q * 16 : q * 16 + 16, :]
            in_s[q, 16:19, :] = own_ref[192 + q * 3 : 192 + q * 3 + 3, :]
            in_s[q, 19:21, :] = gap
            in_s[q, 21:24, :] = own_ref[160 + q * 3 : 160 + q * 3 + 3, :]
            out_s[q, 0:16, :] = far_ref[q * 16 : q * 16 + 16, :]
            out_s[q, 16:19, :] = far_ref[192 + q * 3 : 192 + q * 3 + 3, :]
            out_s[q, 19:21, :] = gap
            out_s[q, 21:24, :] = far_ref[160 + q * 3 : 160 + q * 3 + 3, :]

        def pi(k):
            return in_s[k]

        def po(k):
            return out_s[k]

        gi = [jnp.where(inside, gain(in_s[7 + k]), 0.0) for k in range(3)]
        go = [jnp.where(inside, gain(out_s[7 + k]), 0.0) for k in range(3)]
        outer_gains.append(go)

        def first(g, r, mine, a, b):
            return jnp.where(inside, g * (r + a + b + xy(mine)) - 0.8 * mine, 0.0)

        e0o2 = first(go[2], out_s[6], po(2), po(3), po(1))
        e0o1 = first(go[1], out_s[5], po(1), po(2), po(0))
        e0o0 = first(go[0], out_s[4], po(0), po(1), pi(0))
        e0i0 = first(gi[0], in_s[4], pi(0), po(0), pi(1))
        e0i1 = first(gi[1], in_s[5], pi(1), pi(0), pi(2))
        e1o1 = 1.2 * e0o1 + go[1] * (e0o2 + e0o0 + xy(e0o1))
        e1o0 = 1.2 * e0o0 + go[0] * (e0o1 + e0i0 + xy(e0o0))
        e1i0 = 1.2 * e0i0 + gi[0] * (e0o0 + e0i1 + xy(e0i0))
        e2o0 = 0.2 * e1o0 + e0o0 + go[0] * (e1o1 + e1i0 + xy(e1o0))
        d00 = gi[0] * po(0)
        d10 = 1.2 * d00 + gi[0] * (e0o0 + xy(d00))
        d11 = gi[1] * d00
        d20 = 0.2 * d10 + d00 + gi[0] * (e1o0 + d11 + xy(d10))
        d21 = 0.2 * d11 + gi[1] * (d10 + xy(d11))
        d22 = gi[2] * d11
        d30 = 0.2 * d20 + d00 + gi[0] * (e2o0 + d21 + xy(d20))
        d31 = 0.2 * d21 + gi[1] * (d20 + d22 + xy(d21))
        d32 = 0.2 * d22 + gi[2] * (d21 + xy(d22))
        d33 = gain(dx_ref[side]) * d22[0:16]
        for k, v in enumerate((d30[0:16], d31[0:16], d32[0:16], d33)):
            for b in range(ny // 128):
                t_s[b, pl.ds(4 + k if side == 0 else 3 - k, 16, stride=8), :] = v[:, b * 128 : b * 128 + 128]
    for b in range(ny // 128):
        pd_ref[b * 128 : b * 128 + 128, :] = t_s[b].T

    lane = lax.broadcasted_iota(jnp.int32, (24, 128), 1)
    for wall, (p1_ref, p2_ref, n1_ref, n2_ref) in enumerate(((p1_lo, p2_lo, n1_lo, n2_lo), (p1_hi, p2_hi, n1_hi, n2_hi))):
        for j in range(4):
            y = j if wall == 0 else 7 - j
            big = j if wall == 0 else ny - 1 - j
            gw_ref[wall, j, :, 0:128] = jnp.zeros((24, 128), F32)
            gw_ref[wall, j, 16:17, 0:128] = n1_ref[0, y : y + 1, :]
            gw_ref[wall, j, 17:18, 0:128] = n2_ref[0, y : y + 1, :]
            gw_ref[wall, j, 22:23, 0:128] = p2_ref[0, y : y + 1, :]
            gw_ref[wall, j, 23:24, 0:128] = p1_ref[0, y : y + 1, :]
            acc = jnp.zeros((24, 128), F32)
            for k in range(3):
                acc = jnp.where(lane == 127 - k, outer_gains[0][k][:, big : big + 1], acc)
                acc = jnp.where(lane == k, outer_gains[1][k][:, big : big + 1], acc)
            gw_ref[wall, j, :, 128:256] = acc


def strips(zl, zr, dx, far_l, far_r, x_prev, x_next):
    ny, nz = zl.shape[1], x_prev.shape[2]

    def whole(a):
        return pl.BlockSpec(a.shape, lambda i: (0,) * a.ndim)

    far = x_prev.shape[0] - 1

    def halo(part, at):
        return pl.BlockSpec((1, 8, nz), lambda i: (part, at, 0))

    return pl.pallas_call(
        strip_kernel,
        grid=(1,),
        in_specs=[whole(a) for a in (zl, zr, dx, far_l, far_r)]
        + [halo(0, 48), halo(0, 64), halo(far, 63), halo(far, 79)] * 2,
        out_specs=[pl.BlockSpec((ny, 128), lambda i: (0, 0)), pl.BlockSpec((2, 4, 24, 256), lambda i: (0, 0, 0, 0))],
        out_shape=[sds(ny, 128), sds(2, 4, 24, 256)],
        scratch_shapes=[pltpu.VMEM((10, 24, ny), F32), pltpu.VMEM((10, 24, ny), F32), pltpu.VMEM((ny // 128, 128, 128), F32)],
        compiler_params=params(20),
        cost_estimate=cost(3),
    )(zl, zr, dx, far_l, far_r, *[x_prev] * 4, *[x_next] * 4)


def join_kernel(o_hbm, pd_ref, xp_ref, xn_ref, xl_ref, xr_ref, e1_ref, d_hbm, out_hbm, rim_ref, o_s, tall_s, add_s, d_ref, i_sem, o_sem, d_sem):
    nx, ny, nz = o_hbm.shape
    chunks = ny // CH

    def rows(c):
        return pl.ds(pl.multiple_of(c * CH, CH), CH)

    def i_copy(c):
        return pltpu.make_async_copy(o_hbm.at[:, rows(c), :], o_s.at[:, rows(c), :], i_sem.at[c])

    def o_copy(c):
        return pltpu.make_async_copy(o_s.at[:, rows(c), :], out_hbm.at[:, rows(c), :], o_sem.at[c])

    d_copies = [pltpu.make_async_copy(d_hbm.at[x], d_ref.at[k], d_sem.at[k]) for k, x in enumerate((2, 3, nx - 3, nx - 4))]
    for copy in d_copies:
        copy.start()
    for c in range(chunks):
        i_copy(c).start()
    for k in range(tall_s.shape[0]):
        tall_s[k, 0:8, :] = jnp.zeros((8, nz), F32)
        tall_s[k, ny + 8 : ny + 16, :] = jnp.zeros((8, nz), F32)

    def yz(k, c, mine):
        start = c * CH + 8
        return tall_s[k, pl.ds(start - 1, CH), :] + tall_s[k, pl.ds(start + 1, CH), :] + span(mine)

    def each(c, side, far, own, stage):
        r = rows(c)
        t = pl.ds(pl.multiple_of(c * CH + 8, 8), CH)
        b = side * 9
        part = c // 2
        low = (c % 2) * CH

        def of(ref, k):
            return ref[part, pl.ds(pl.multiple_of(k * 128 + low, CH), CH), :]

        gm1, gm2, g0, g1 = of(far, 3), of(far, 4), of(own, 3), of(own, 4)
        if stage == 0:
            tall_s[b, t, :] = of(far, 1) + gm1 * of(own, 0)
            tall_s[b + 1, t, :] = of(far, 2)
            tall_s[b + 2, t, :] = g0 * of(far, 0)
            return
        em1, em2, d00 = tall_s[b, t, :], tall_s[b + 1, t, :], tall_s[b + 2, t, :]
        if stage == 1:
            tall_s[b + 3, t, :] = 1.2 * em1 + gm1 * (em2 + of(own, 1) + d00 + yz(b, c, em1))
            tall_s[b + 4, t, :] = 1.2 * em2 + gm2 * (em1 + yz(b + 1, c, em2))
            tall_s[b + 5, t, :] = 1.2 * d00 + g0 * (em1 + yz(b + 2, c, d00))
            tall_s[b + 6, t, :] = g1 * d00
            return
        e1m1, e1m2, d10, d11 = (tall_s[b + k, t, :] for k in (3, 4, 5, 6))
        g2 = gain(d_ref[2 * side, r, :])
        if stage == 2:
            e2m1 = 0.2 * e1m1 + em1 + gm1 * (e1m2 + e1_ref[side, r, :] + d10 + yz(b + 3, c, e1m1))
            d20 = 0.2 * d10 + d00 + g0 * (e1m1 + d11 + yz(b + 5, c, d10))
            d21 = 0.2 * d11 + g1 * (d10 + yz(b + 6, c, d11))
            d22 = g2 * d11
            tall_s[b, t, :] = e2m1
            tall_s[b + 1, t, :] = d20
            tall_s[b + 7, t, :] = d21
            tall_s[b + 8, t, :] = d22
            return
        e2m1, d20, d21, d22 = (tall_s[b + k, t, :] for k in (0, 1, 7, 8))
        g3 = gain(d_ref[2 * side + 1, r, :])
        d30 = 0.2 * d20 + d00 + g0 * (e2m1 + d21 + yz(b + 1, c, d20))
        d31 = 0.2 * d21 + g1 * (d20 + d22 + yz(b + 7, c, d21))
        d32 = 0.2 * d22 + g2 * (d21 + yz(b + 8, c, d22))
        d33 = g3 * d22
        for k, v in enumerate((d30, d31, d32, d33)):
            add_s[k if side == 0 else 7 - k, :, :] = v

    def stage_loop(stage):
        def body(c, carry):
            each(c, 0, xp_ref, xl_ref, stage)
            each(c, 1, xn_ref, xr_ref, stage)
            return carry

        lax.fori_loop(0, chunks, body, 0)

    stage_loop(0)
    stage_loop(1)
    for copy in d_copies:
        copy.wait()
    stage_loop(2)

    lane = lax.broadcasted_iota(jnp.int32, (CH, nz), 1)
    edge = (lane < 4) | (lane > nz - 5)

    def final(c, carry):
        each(c, 0, xp_ref, xl_ref, 3)
        each(c, 1, xn_ref, xr_ref, 3)
        i_copy(c).wait()
        r = rows(c)
        packed = pd_ref[r, :]
        for x in range(nx):
            strip = jnp.where(edge, pltpu.roll(packed, (128 - 4 - 8 * x) % 128, 1), 0.0)
            v = o_s[x, r, :] + strip
            if x < 4:
                v = v + add_s[x]
            if x >= nx - 4:
                v = v + add_s[x - nx + 8]
            o_s[x, r, :] = v
        o_copy(c).start()
        return carry

    lax.fori_loop(0, chunks, final, 0)
    for x in range(nx):
        rim_ref[0, x] = o_s[x, 0:8, :]
        rim_ref[1, x] = o_s[x, ny - 8 : ny, :]
    for c in range(chunks):
        o_copy(c).wait()


def join(out, packed, x_prev, x_next, x_left, x_right, e1, d):
    nx, ny, nz = out.shape
    chunks = ny // CH
    return pl.pallas_call(
        join_kernel,
        out_shape=[sds(nx, ny, nz), sds(2, nx, 8, nz)],
        in_specs=[HBM] + [VMEM] * 6 + [HBM],
        out_specs=[HBM, VMEM],
        scratch_shapes=[
            pltpu.VMEM((nx, ny, nz), F32),
            pltpu.VMEM((18, ny + 16, nz), F32),
            pltpu.VMEM((8, CH, nz), F32),
            pltpu.VMEM((4, ny, nz), F32),
            pltpu.SemaphoreType.DMA((chunks,)),
            pltpu.SemaphoreType.DMA((chunks,)),
            pltpu.SemaphoreType.DMA((4,)),
        ],
        input_output_aliases={0: 0},
        compiler_params=params(26),
        cost_estimate=cost(9),
    )(out, packed, x_prev, x_next, x_left, x_right, e1, d)


def finish_kernel(o_hbm, rim_ref, w_ref, wp_ref, wn_ref, l_ref, r_ref, gw_ref, gr_ref, out_hbm, new_s, sem):
    lane = lax.broadcasted_iota(jnp.int32, (24, 128), 1)
    half = lax.broadcasted_iota(jnp.int32, (8, 128), 0)
    ny = out_hbm.shape[1]
    copies = []
    for wall in range(2):
        at = wall * 16

        def rows(mine, before, after):
            return jnp.concatenate([mine, jnp.where(half < 4, after[0:8], before[8:16])], axis=0)

        def take(ref, base):
            return ref[base + at : base + at + 16, :]

        centre = rows(take(w_ref, 0), take(wp_ref, 0), take(wn_ref, 0))
        left = rows(take(l_ref, 0), take(l_ref, 32), take(l_ref, 64))
        right = rows(take(r_ref, 0), take(r_ref, 32), take(r_ref, 64))
        beyond = jnp.where(lane < 3, right, jnp.where(lane > 124, left, 0.0))
        w = jnp.concatenate([centre, beyond], axis=1)
        g = []
        for j in range(4):
            mine = gr_ref[wall, :, j if wall == 0 else 7 - j, :]
            halo = gw_ref[wall, j]
            g.append(jnp.concatenate([jnp.concatenate([mine, halo[16:24, 0:128]], axis=0), halo[:, 128:256]], axis=1))

        def xz(v):
            return pltpu.roll(v, 1, 0) + pltpu.roll(v, 23, 0) + pltpu.roll(v, 1, 1) + pltpu.roll(v, 255, 1)

        e0 = g[0] * w
        a0 = 1.2 * e0 + g[0] * xz(e0)
        a1 = g[1] * e0
        b0 = 0.2 * a0 + e0 + g[0] * (a1 + xz(a0))
        b1 = 0.2 * a1 + g[1] * (a0 + xz(a1))
        b2 = g[2] * a1
        c0 = 0.2 * b0 + e0 + g[0] * (b1 + xz(b0))
        c1 = 0.2 * b1 + g[1] * (b0 + b2 + xz(b1))
        c2 = 0.2 * b2 + g[2] * (b1 + xz(b2))
        c3 = g[3] * b2
        new_s[wall] = rim_ref[wall]
        for j, v in enumerate((c0, c1, c2, c3)):
            y = j if wall == 0 else 7 - j
            new_s[wall, :, y, :] = new_s[wall, :, y, :] + v[0:16, 0:128]
        first = 0 if wall == 0 else ny - 8
        copies.append(pltpu.make_async_copy(new_s.at[wall], out_hbm.at[:, first : first + 8, :], sem.at[wall]))
        copies[wall].start()
    for copy in copies:
        copy.wait()


def finish(out, edge_rows, w, w_prev, w_next, left, right, gw, g_rows):
    nx, ny, nz = out.shape
    return pl.pallas_call(
        finish_kernel,
        out_shape=sds(nx, ny, nz),
        in_specs=[HBM] + [VMEM] * 8,
        out_specs=HBM,
        scratch_shapes=[pltpu.VMEM((2, nx, 8, nz), F32), pltpu.SemaphoreType.DMA((2,))],
        input_output_aliases={0: 0},
        compiler_params=params(8),
        cost_estimate=cost(2),
    )(out, edge_rows, w, w_prev, w_next, left, right, gw, g_rows)


def trio_kernel(a_ref, b_ref, c_ref, out_ref):
    for k, ref in enumerate((a_ref, b_ref, c_ref)):
        out_ref[k * 32 : k * 32 + 32, :] = ref[...]


def trio_of(a, b, c):
    return pl.pallas_call(trio_kernel, out_shape=sds(96, 128), in_specs=[VMEM] * 3, out_specs=VMEM, compiler_params=params(4), cost_estimate=cost(1))(a, b, c)


def shift(block, axis, distance):
    size = lax.axis_size(axis)
    return lax.ppermute(block, axis, [((i - distance) % size, i) for i in range(size)])


def local(right_side, pressure, diagonal, corrections, wall_cells, owners):
    n_dev = lax.axis_size("gx") * lax.axis_size("gz")
    zl, zr, dx, x_left, x_right = edges(pressure, right_side, diagonal)
    corrections, x_left = lax.optimization_barrier((corrections, x_left))
    slots = pack(corrections, wall_cells, owners, n_dev)
    got = lax.all_to_all(slots.reshape(n_dev, 8, 128), AXES, split_axis=0, concat_axis=0, tiled=True).reshape(n_dev * 8, 128)
    x_prev = shift(x_right, "gx", 1)
    x_next = shift(x_left, "gx", -1)
    out, e1, g_rows = main_part(pressure, right_side, diagonal, x_left)
    x_prev, x_next, e1 = lax.optimization_barrier((x_prev, x_next, e1))
    zl, zr = relay(zl, zr, x_prev, x_next)
    far_l = shift(zr, "gz", 1)
    far_r = shift(zl, "gz", -1)
    w = wall_sums(got)
    w_prev = shift(w, "gx", 1)
    w_next = shift(w, "gx", -1)
    packed, gw = strips(zl, zr, dx, far_l, far_r, x_prev, x_next)
    w_prev, w_next, packed = lax.optimization_barrier((w_prev, w_next, packed))
    trio = trio_of(w, w_prev, w_next)
    left = shift(trio, "gz", 1)
    right = shift(trio, "gz", -1)
    out, edge_rows = join(out, packed, x_prev, x_next, x_left, x_right, e1, diagonal)
    return finish(out, edge_rows, w, w_prev, w_next, left, right, gw, g_rows)


def solution(mesh):
    in_specs = (
        P("gx", None, "gz"),
        P("gx", None, "gz"),
        P("gx", None, "gz"),
        P(AXES, None),
        P(AXES, None),
        P(AXES, None),
    )
    return jax.shard_map(local, mesh=mesh, in_specs=in_specs, out_specs=P("gx", None, "gz"), check_vma=False)
```

```python
import jax
import jax.numpy as jnp
from jax import lax
from jax.experimental import pallas as pl
from jax.experimental.pallas import tpu as pltpu
from jax.sharding import PartitionSpec as P

F32 = jnp.float32
BF16 = jnp.bfloat16
AXES = ("gx", "gz")
VMEM = pl.BlockSpec(memory_space=pltpu.VMEM)
HBM = pl.BlockSpec(memory_space=pl.ANY)
MIB = 2**20


def sds(*shape):
    return jax.ShapeDtypeStruct(shape, F32)


def params(mib):
    return pltpu.CompilerParams(vmem_limit_bytes=mib * MIB)


def cost(us):
    return pl.CostEstimate(flops=0, transcendentals=0, bytes_accessed=us * 3_000_000)


def gain(diag):
    return 0.8 / (6.0 + diag)


def pack_kernel(corr_ref, cell_ref, own_ref, out_ref):
    blocks = corr_ref.shape[0]
    rows = out_ref.shape[0]
    own_row = own_ref[...].astype(F32)
    row = lax.broadcasted_iota(jnp.int32, (blocks, blocks), 0)
    col = lax.broadcasted_iota(jnp.int32, (blocks, blocks), 1)
    own = jnp.sum(jnp.where(row == col, own_row, 0.0), axis=1, keepdims=True)
    same = jnp.where((own == own_row) & (row < col), 1.0, 0.0)
    slot = own_row * 8.0 + jnp.sum(same, axis=0, keepdims=True)
    index = lax.broadcasted_iota(jnp.int32, (rows, blocks), 0).astype(F32)
    put_v = jnp.where(index == slot, 1.0, 0.0).astype(BF16)
    put_c = jnp.where(index == slot + 4.0, 1.0, 0.0).astype(BF16)
    vals = corr_ref[...]
    high = vals.astype(BF16)
    rest = vals - high.astype(F32)
    mid = rest.astype(BF16)
    cells = cell_ref[...]
    major = (cells // 128).astype(F32).astype(BF16)
    minor = (cells % 128).astype(F32).astype(BF16)

    def put(place, first, second):
        return jnp.dot(place, jnp.concatenate([first, second], axis=1), preferred_element_type=F32)

    value = put(put_v, high, mid)
    cell = put(put_c, major, minor)
    out_ref[...] = value[:, 0:128] + value[:, 128:256] + (cell[:, 0:128] * 128.0 + cell[:, 128:256])


def pack(corrections, wall_cells, owners, n_dev):
    return pl.pallas_call(
        pack_kernel,
        out_shape=sds(n_dev * 8, corrections.shape[1]),
        in_specs=[VMEM] * 3,
        out_specs=VMEM,
        compiler_params=params(56),
        cost_estimate=cost(3),
    )(corrections, wall_cells, owners.reshape(1, -1))


def wall_kernel(got_ref, w_ref, high_s, low_s, major_s, minor_s):
    rows = got_ref.shape[0]
    got = got_ref[...]
    high = got.astype(BF16).astype(F32)
    high_s[...] = high
    low_s[...] = got - high
    major = jnp.floor(got * (1.0 / 128.0))
    major_s[...] = major
    minor_s[...] = got - major * 128.0
    many = 16
    row_id = lax.broadcasted_iota(jnp.int32, (32, 128), 0).astype(F32)
    col_id = lax.broadcasted_iota(jnp.int32, (128, 128), 0).astype(F32)

    def spread(ref, at, n):
        return jnp.broadcast_to(ref[pl.ds(at, 1), :], (n, 128))

    def step(i, total):
        lefts, rights = [], []
        for k in range(many):
            at = i * (2 * many) + (k // 4) * 8 + k % 4
            hit = spread(major_s, at + 4, 32) == row_id
            top = jnp.where(hit, spread(high_s, at, 32), 0.0).astype(BF16)
            end = jnp.where(hit, spread(low_s, at, 32), 0.0).astype(BF16)
            lefts.append(jnp.concatenate([top, end], axis=0))
            hot = spread(minor_s, at + 4, 128) == col_id
            rights.append(jnp.where(hot, 1.0, 0.0).astype(BF16))
        left = jnp.concatenate(lefts, axis=1)
        right = jnp.concatenate(rights, axis=1)
        return total + lax.dot_general(
            left, right, (((1,), (1,)), ((), ())), preferred_element_type=F32
        )

    total = lax.fori_loop(0, rows // (2 * many), step, jnp.zeros((64, 128), F32), unroll=8)
    w_ref[...] = total[:32] + total[32:]


def wall_sums(got):
    scratch = [pltpu.VMEM(got.shape, F32)] * 4
    return pl.pallas_call(
        wall_kernel,
        out_shape=sds(32, 128),
        in_specs=[VMEM],
        out_specs=VMEM,
        scratch_shapes=scratch,
        compiler_params=params(16),
        cost_estimate=cost(7),
    )(got)


def edge_kernel(p_ref, pu_ref, pd_ref, r_ref, d_ref, zl_ref, zr_ref, dx_ref, xl_ref, xr_ref, pk_s, t_s):
    i = pl.program_id(0)
    lane = lax.broadcasted_iota(jnp.int32, (32, 128), 1)
    small = 640
    base = 0
    for which, (ref, depth) in enumerate(((p_ref, 4), (r_ref, 3), (d_ref, 3))):
        for sub in range(4):
            acc = None
            for x in range(16):
                moved = pltpu.roll(ref[x, sub * 32 : sub * 32 + 32, :], (x * 8 + 4) % 128, 1)
                acc = moved if acc is None else jnp.where(lane // 8 == x, moved, acc)
            pk_s[which, sub * 32 : sub * 32 + 32, :] = acc
        t_s[which] = pk_s[which].T
        for k in range(4):
            left = t_s[which, pl.ds(4 + k, 16, stride=8), :]
            right = t_s[which, pl.ds(3 - k, 16, stride=8), :]
            if k < depth:
                q = base + k
                zl_ref[q * 16 : q * 16 + 16, :] = left
                zr_ref[q * 16 : q * 16 + 16, :] = right
                for side, v in enumerate((left, right)):
                    at = small + side * 32 + q * 3
                    xl_ref[0, at : at + 3, :] = v[0:3]
                    xr_ref[0, at : at + 3, :] = v[13:16]
            elif which == 2:
                dx_ref[0] = left
                dx_ref[1] = right
        base += depth

    row = lax.broadcasted_iota(jnp.int32, (128, 128), 0)
    col = lax.broadcasted_iota(jnp.int32, (128, 128), 1)
    first = jnp.where(i > 0, 1.0, 0.0)
    last = jnp.where(i < pl.num_programs(0) - 1, 1.0, 0.0)

    def level0(x, nbrs):
        mine = p_ref[x]
        up = jnp.where(row == 0, pu_ref[x, 7:8, :] * first, pltpu.roll(mine, 1, 0))
        down = jnp.where(row == 127, pd_ref[x, 0:1, :] * last, pltpu.roll(mine, 127, 0))
        near = up + down
        near = near + jnp.where(col == 0, 0.0, pltpu.roll(mine, 1, 1))
        near = near + jnp.where(col == 127, 0.0, pltpu.roll(mine, 127, 1))
        for n in nbrs:
            near = near + p_ref[n]
        g = gain(d_ref[x])
        return g * (r_ref[x] + near) - 0.8 * mine, g

    for ref, edge, inner, third in ((xl_ref, 0, 1, 2), (xr_ref, 15, 14, 13)):
        ref[0, 0:128, :] = p_ref[edge]
        e, g = level0(edge, (inner,))
        ref[0, 128:256, :] = e
        ref[0, 384:512, :] = g
        e, g = level0(inner, (edge, third))
        ref[0, 256:384, :] = e
        ref[0, 512:640, :] = g
        for side in range(2):
            ref[0, small + side * 32 + 30 : small + side * 32 + 32, :] = jnp.zeros((2, 128), F32)


def edges(p, r, d):
    nx, ny, nz = p.shape
    whole = pl.BlockSpec((nx, 128, 128), lambda i: (0, i, 0))
    above = pl.BlockSpec((nx, 8, 128), lambda i: (0, jnp.maximum(16 * i - 1, 0), 0))
    under = pl.BlockSpec((nx, 8, 128), lambda i: (0, jnp.minimum(16 * i + 16, ny // 8 - 1), 0))
    strip = pl.BlockSpec((160, 128), lambda i: (0, i))
    return pl.pallas_call(
        edge_kernel,
        grid=(ny // 128,),
        in_specs=[whole, above, under, whole, whole],
        out_specs=[
            strip,
            strip,
            pl.BlockSpec((2, nx, 128), lambda i: (0, 0, i)),
            pl.BlockSpec((1, 704, nz), lambda i: (i, 0, 0)),
            pl.BlockSpec((1, 704, nz), lambda i: (i, 0, 0)),
        ],
        out_shape=[sds(224, ny), sds(224, ny), sds(2, nx, ny), sds(ny // 128, 704, nz), sds(ny // 128, 704, nz)],
        scratch_shapes=[pltpu.VMEM((3, 128, 128), F32), pltpu.VMEM((3, 128, 128), F32)],
        compiler_params=params(56),
        cost_estimate=cost(9),
    )(p, p, p, r, d)


def relay_kernel(zl_in, zr_in, xp_ref, xn_ref, zl_ref, zr_ref, sem):
    copies = []
    for side, z in enumerate((zl_ref, zr_ref)):
        for k, x in enumerate((xp_ref, xn_ref)):
            for b in range(x.shape[0]):
                at = 640 + side * 32
                lanes = z.at[160 + 32 * k : 192 + 32 * k, b * 128 : b * 128 + 128]
                copies.append(pltpu.make_async_copy(x.at[b, at : at + 32, :], lanes, sem.at[len(copies)]))
    for c in copies:
        c.start()
    for c in copies:
        c.wait()


def relay(zl, zr, x_prev, x_next):
    return pl.pallas_call(
        relay_kernel,
        out_shape=[sds(*zl.shape), sds(*zr.shape)],
        in_specs=[HBM] * 4,
        out_specs=[HBM] * 2,
        scratch_shapes=[pltpu.SemaphoreType.DMA((4 * x_prev.shape[0],))],
        input_output_aliases={0: 0, 1: 1},
        compiler_params=params(4),
        cost_estimate=cost(1),
    )(zl, zr, x_prev, x_next)


CH = 64
MAIN_CH = 128


def span(mine):
    col = lax.broadcasted_iota(jnp.int32, mine.shape, 1)
    near = jnp.where(col == 0, 0.0, pltpu.roll(mine, 1, 1))
    return near + jnp.where(col == mine.shape[1] - 1, 0.0, pltpu.roll(mine, mine.shape[1] - 1, 1))


def beside(n):
    a = lax.broadcasted_iota(jnp.int32, (2 * n, n), 0) % n
    b = lax.broadcasted_iota(jnp.int32, (2 * n, n), 1)
    return jnp.where((a == b + 1) | (a == b - 1), 1.0, 0.0).astype(BF16)


def spans(v, place):
    high = v.astype(BF16)
    low = (v - high.astype(F32)).astype(BF16)
    return jnp.dot(jnp.concatenate([high, low], axis=1), place, preferred_element_type=F32)


def main_kernel(p_hbm, r_hbm, d_hbm, after_ref, out_hbm, e1_hbm, gr_ref, p_s, g_s, e0_s, e1_s, e2_s, p_sem, r_sem, d_sem, o_sem, e_sem):
    nx, ny, nz = p_hbm.shape
    chunks = ny // MAIN_CH

    def rows(c):
        return pl.ds(pl.multiple_of(c * MAIN_CH, MAIN_CH), MAIN_CH)

    def held(c):
        return pl.ds(pl.multiple_of(8 + c * MAIN_CH, 8), MAIN_CH)

    def p_copy(c):
        return pltpu.make_async_copy(p_hbm.at[:, rows(c), :], p_s.at[:, held(c), :], p_sem.at[c])

    def r_copy(c):
        return pltpu.make_async_copy(r_hbm.at[:, rows(c), :], e0_s.at[:, held(c), :], r_sem.at[c])

    def d_copy(c):
        return pltpu.make_async_copy(d_hbm.at[:, rows(c), :], g_s.at[:, rows(c), :], d_sem.at[c])

    def o_copy(c):
        return pltpu.make_async_copy(p_s.at[:, held(c), :], out_hbm.at[:, rows(c), :], o_sem.at[c])

    p_copy(0).start()
    for c in range(chunks):
        r_copy(c).start()
        d_copy(c).start()
        if c + 1 < chunks:
            p_copy(c + 1).start()
    for ref in (p_s, e0_s, e1_s, e2_s):
        for x in range(nx):
            ref[x, 0:8, :] = jnp.zeros((8, nz), F32)
            ref[x, ny + 8 : ny + 16, :] = jnp.zeros((8, nz), F32)
    nothing = jnp.zeros((MAIN_CH, nz), F32)
    place = beside(nz)

    def sweep(src, c, update):
        start = c * MAIN_CH + 8
        here = pl.ds(pl.multiple_of(start, 8), MAIN_CH)
        before, mine = nothing, src[0, here, :]
        for x in range(nx):
            after = src[x + 1, here, :] if x + 1 < nx else nothing
            if x % 2 == 0 and x % 8 == 0:
                four = jnp.concatenate([src[x + 2 * q, here, :] for q in range(4)], axis=0)
                sums = spans(four, place).reshape(4, MAIN_CH, nz)
            near = before + after + src[x, pl.ds(start - 1, MAIN_CH), :] + src[x, pl.ds(start + 1, MAIN_CH), :]
            update(x, mine, near + (sums[x % 8 // 2] if x % 2 == 0 else span(mine)), here)
            before, mine = mine, after

    def level0(c):
        here_g = rows(c)

        def update(x, mine, near, here):
            g = gain(g_s[x, here_g, :])
            g_s[x, here_g, :] = g
            e0_s[x, here, :] = g * (e0_s[x, here, :] + near) - 0.8 * mine

        sweep(p_s, c, update)

    def level1(c):
        here_g = rows(c)

        def update(x, mine, near, here):
            e1_s[x, here, :] = 1.2 * mine + g_s[x, here_g, :] * near

        sweep(e0_s, c, update)

    def level2(c):
        here_g = rows(c)

        def update(x, mine, near, here):
            e2_s[x, here, :] = 0.2 * mine + e0_s[x, here, :] + g_s[x, here_g, :] * near

        sweep(e1_s, c, update)

    def level3(c):
        here_g = rows(c)

        def update(x, mine, near, here):
            e3 = 0.2 * mine + e0_s[x, here, :] + g_s[x, here_g, :] * near
            p_s[x, here, :] = p_s[x, here, :] + e3

        sweep(e2_s, c, update)
        o_copy(c).start()

    p_copy(0).wait()

    def turn(c, carry):
        @pl.when(c < chunks)
        def _():
            @pl.when(c + 1 < chunks)
            def _():
                p_copy(c + 1).wait()

            r_copy(c).wait()
            d_copy(c).wait()
            level0(c)

        for k, level in ((1, level1), (2, level2), (3, level3)):

            @pl.when((c >= k) & (c - k < chunks))
            def _(k=k, level=level):
                level(c - k)

        return carry

    lax.fori_loop(0, chunks + 3, turn, 0)
    sent = [pltpu.make_async_copy(e1_s.at[x, pl.ds(8, ny), :], e1_hbm.at[k], e_sem.at[k]) for k, x in enumerate((0, nx - 1))]
    for s in sent:
        s.start()
    for x in range(nx):
        gr_ref[0, x] = g_s[x, 0:8, :]
        gr_ref[1, x] = g_s[x, ny - 8 : ny, :]
    for s in sent:
        s.wait()
    for c in range(chunks):
        o_copy(c).wait()


def main_part(p, r, d, after):
    nx, ny, nz = p.shape
    chunks = ny // MAIN_CH
    tall = pltpu.VMEM((nx, ny + 16, nz), F32)
    dma = pltpu.SemaphoreType.DMA
    return pl.pallas_call(
        main_kernel,
        out_shape=[sds(nx, ny, nz), sds(2, ny, nz), sds(2, nx, 8, nz)],
        in_specs=[HBM] * 4,
        out_specs=[HBM, HBM, VMEM],
        scratch_shapes=[tall, pltpu.VMEM((nx, ny, nz), F32), tall, tall, tall, dma((chunks,)), dma((chunks,)), dma((chunks,)), dma((chunks,)), dma((2,))],
        compiler_params=params(56),
        cost_estimate=cost(12),
    )(p, r, d, after)


def strip_kernel(zl_ref, zr_ref, dx_ref, fl_ref, fr_ref, p1_lo, p2_lo, p1_hi, p2_hi, n1_lo, n2_lo, n1_hi, n2_hi, pd_ref, gw_ref, in_s, out_s, t_s):
    ny = zl_ref.shape[1]
    row = lax.broadcasted_iota(jnp.int32, (24, ny), 0)
    col = lax.broadcasted_iota(jnp.int32, (24, ny), 1)
    inside = (row < 18) | (row > 21)
    gap = jnp.zeros((2, ny), F32)

    def xy(v):
        near = pltpu.roll(v, 1, 0) + pltpu.roll(v, 23, 0)
        near = near + jnp.where(col == 0, 0.0, pltpu.roll(v, 1, 1))
        return near + jnp.where(col == ny - 1, 0.0, pltpu.roll(v, ny - 1, 1))

    outer_gains = []
    for side, (own_ref, far_ref) in enumerate(((zl_ref, fl_ref), (zr_ref, fr_ref))):
        for q in range(10):
            in_s[q, 0:16, :] = own_ref[q * 16 : q * 16 + 16, :]
            in_s[q, 16:19, :] = own_ref[192 + q * 3 : 192 + q * 3 + 3, :]
            in_s[q, 19:21, :] = gap
            in_s[q, 21:24, :] = own_ref[160 + q * 3 : 160 + q * 3 + 3, :]
            out_s[q, 0:16, :] = far_ref[q * 16 : q * 16 + 16, :]
            out_s[q, 16:19, :] = far_ref[192 + q * 3 : 192 + q * 3 + 3, :]
            out_s[q, 19:21, :] = gap
            out_s[q, 21:24, :] = far_ref[160 + q * 3 : 160 + q * 3 + 3, :]

        def pi(k):
            return in_s[k]

        def po(k):
            return out_s[k]

        gi = [jnp.where(inside, gain(in_s[7 + k]), 0.0) for k in range(3)]
        go = [jnp.where(inside, gain(out_s[7 + k]), 0.0) for k in range(3)]
        outer_gains.append(go)

        def first(g, r, mine, a, b):
            return jnp.where(inside, g * (r + a + b + xy(mine)) - 0.8 * mine, 0.0)

        e0o2 = first(go[2], out_s[6], po(2), po(3), po(1))
        e0o1 = first(go[1], out_s[5], po(1), po(2), po(0))
        e0o0 = first(go[0], out_s[4], po(0), po(1), pi(0))
        e0i0 = first(gi[0], in_s[4], pi(0), po(0), pi(1))
        e0i1 = first(gi[1], in_s[5], pi(1), pi(0), pi(2))
        e1o1 = 1.2 * e0o1 + go[1] * (e0o2 + e0o0 + xy(e0o1))
        e1o0 = 1.2 * e0o0 + go[0] * (e0o1 + e0i0 + xy(e0o0))
        e1i0 = 1.2 * e0i0 + gi[0] * (e0o0 + e0i1 + xy(e0i0))
        e2o0 = 0.2 * e1o0 + e0o0 + go[0] * (e1o1 + e1i0 + xy(e1o0))
        d00 = gi[0] * po(0)
        d10 = 1.2 * d00 + gi[0] * (e0o0 + xy(d00))
        d11 = gi[1] * d00
        d20 = 0.2 * d10 + d00 + gi[0] * (e1o0 + d11 + xy(d10))
        d21 = 0.2 * d11 + gi[1] * (d10 + xy(d11))
        d22 = gi[2] * d11
        d30 = 0.2 * d20 + d00 + gi[0] * (e2o0 + d21 + xy(d20))
        d31 = 0.2 * d21 + gi[1] * (d20 + d22 + xy(d21))
        d32 = 0.2 * d22 + gi[2] * (d21 + xy(d22))
        d33 = gain(dx_ref[side]) * d22[0:16]
        for k, v in enumerate((d30[0:16], d31[0:16], d32[0:16], d33)):
            for b in range(ny // 128):
                t_s[b, pl.ds(4 + k if side == 0 else 3 - k, 16, stride=8), :] = v[:, b * 128 : b * 128 + 128]
    for b in range(ny // 128):
        pd_ref[b * 128 : b * 128 + 128, :] = t_s[b].T

    lane = lax.broadcasted_iota(jnp.int32, (24, 128), 1)
    for wall, (p1_ref, p2_ref, n1_ref, n2_ref) in enumerate(((p1_lo, p2_lo, n1_lo, n2_lo), (p1_hi, p2_hi, n1_hi, n2_hi))):
        for j in range(4):
            y = j if wall == 0 else 7 - j
            big = j if wall == 0 else ny - 1 - j
            gw_ref[wall, j, :, 0:128] = jnp.zeros((24, 128), F32)
            gw_ref[wall, j, 16:17, 0:128] = n1_ref[0, y : y + 1, :]
            gw_ref[wall, j, 17:18, 0:128] = n2_ref[0, y : y + 1, :]
            gw_ref[wall, j, 22:23, 0:128] = p2_ref[0, y : y + 1, :]
            gw_ref[wall, j, 23:24, 0:128] = p1_ref[0, y : y + 1, :]
            acc = jnp.zeros((24, 128), F32)
            for k in range(3):
                acc = jnp.where(lane == 127 - k, outer_gains[0][k][:, big : big + 1], acc)
                acc = jnp.where(lane == k, outer_gains[1][k][:, big : big + 1], acc)
            gw_ref[wall, j, :, 128:256] = acc


def strips(zl, zr, dx, far_l, far_r, x_prev, x_next):
    ny, nz = zl.shape[1], x_prev.shape[2]

    def whole(a):
        return pl.BlockSpec(a.shape, lambda i: (0,) * a.ndim)

    far = x_prev.shape[0] - 1

    def halo(part, at):
        return pl.BlockSpec((1, 8, nz), lambda i: (part, at, 0))

    return pl.pallas_call(
        strip_kernel,
        grid=(1,),
        in_specs=[whole(a) for a in (zl, zr, dx, far_l, far_r)]
        + [halo(0, 48), halo(0, 64), halo(far, 63), halo(far, 79)] * 2,
        out_specs=[pl.BlockSpec((ny, 128), lambda i: (0, 0)), pl.BlockSpec((2, 4, 24, 256), lambda i: (0, 0, 0, 0))],
        out_shape=[sds(ny, 128), sds(2, 4, 24, 256)],
        scratch_shapes=[pltpu.VMEM((10, 24, ny), F32), pltpu.VMEM((10, 24, ny), F32), pltpu.VMEM((ny // 128, 128, 128), F32)],
        compiler_params=params(20),
        cost_estimate=cost(3),
    )(zl, zr, dx, far_l, far_r, *[x_prev] * 4, *[x_next] * 4)


def join_kernel(o_hbm, pd_ref, xp_ref, xn_ref, xl_ref, xr_ref, e1_ref, d_hbm, out_hbm, rim_ref, o_s, tall_s, add_s, d_ref, i_sem, o_sem, d_sem):
    nx, ny, nz = o_hbm.shape
    chunks = ny // CH

    def rows(c):
        return pl.ds(pl.multiple_of(c * CH, CH), CH)

    def i_copy(c):
        return pltpu.make_async_copy(o_hbm.at[:, rows(c), :], o_s.at[:, rows(c), :], i_sem.at[c])

    def o_copy(c):
        return pltpu.make_async_copy(o_s.at[:, rows(c), :], out_hbm.at[:, rows(c), :], o_sem.at[c])

    d_copies = [pltpu.make_async_copy(d_hbm.at[x], d_ref.at[k], d_sem.at[k]) for k, x in enumerate((2, 3, nx - 3, nx - 4))]
    for copy in d_copies:
        copy.start()
    for c in range(chunks):
        i_copy(c).start()
    for k in range(tall_s.shape[0]):
        tall_s[k, 0:8, :] = jnp.zeros((8, nz), F32)
        tall_s[k, ny + 8 : ny + 16, :] = jnp.zeros((8, nz), F32)

    def yz(k, c, mine):
        start = c * CH + 8
        return tall_s[k, pl.ds(start - 1, CH), :] + tall_s[k, pl.ds(start + 1, CH), :] + span(mine)

    def each(c, side, far, own, stage):
        r = rows(c)
        t = pl.ds(pl.multiple_of(c * CH + 8, 8), CH)
        b = side * 9
        part = c // 2
        low = (c % 2) * CH

        def of(ref, k):
            return ref[part, pl.ds(pl.multiple_of(k * 128 + low, CH), CH), :]

        gm1, gm2, g0, g1 = of(far, 3), of(far, 4), of(own, 3), of(own, 4)
        if stage == 0:
            tall_s[b, t, :] = of(far, 1) + gm1 * of(own, 0)
            tall_s[b + 1, t, :] = of(far, 2)
            tall_s[b + 2, t, :] = g0 * of(far, 0)
            return
        em1, em2, d00 = tall_s[b, t, :], tall_s[b + 1, t, :], tall_s[b + 2, t, :]
        if stage == 1:
            tall_s[b + 3, t, :] = 1.2 * em1 + gm1 * (em2 + of(own, 1) + d00 + yz(b, c, em1))
            tall_s[b + 4, t, :] = 1.2 * em2 + gm2 * (em1 + yz(b + 1, c, em2))
            tall_s[b + 5, t, :] = 1.2 * d00 + g0 * (em1 + yz(b + 2, c, d00))
            tall_s[b + 6, t, :] = g1 * d00
            return
        e1m1, e1m2, d10, d11 = (tall_s[b + k, t, :] for k in (3, 4, 5, 6))
        g2 = gain(d_ref[2 * side, r, :])
        if stage == 2:
            e2m1 = 0.2 * e1m1 + em1 + gm1 * (e1m2 + e1_ref[side, r, :] + d10 + yz(b + 3, c, e1m1))
            d20 = 0.2 * d10 + d00 + g0 * (e1m1 + d11 + yz(b + 5, c, d10))
            d21 = 0.2 * d11 + g1 * (d10 + yz(b + 6, c, d11))
            d22 = g2 * d11
            tall_s[b, t, :] = e2m1
            tall_s[b + 1, t, :] = d20
            tall_s[b + 7, t, :] = d21
            tall_s[b + 8, t, :] = d22
            return
        e2m1, d20, d21, d22 = (tall_s[b + k, t, :] for k in (0, 1, 7, 8))
        g3 = gain(d_ref[2 * side + 1, r, :])
        d30 = 0.2 * d20 + d00 + g0 * (e2m1 + d21 + yz(b + 1, c, d20))
        d31 = 0.2 * d21 + g1 * (d20 + d22 + yz(b + 7, c, d21))
        d32 = 0.2 * d22 + g2 * (d21 + yz(b + 8, c, d22))
        d33 = g3 * d22
        for k, v in enumerate((d30, d31, d32, d33)):
            add_s[k if side == 0 else 7 - k, :, :] = v

    def stage_loop(stage):
        def body(c, carry):
            each(c, 0, xp_ref, xl_ref, stage)
            each(c, 1, xn_ref, xr_ref, stage)
            return carry

        lax.fori_loop(0, chunks, body, 0)

    stage_loop(0)
    stage_loop(1)
    for copy in d_copies:
        copy.wait()
    stage_loop(2)

    lane = lax.broadcasted_iota(jnp.int32, (CH, nz), 1)
    edge = (lane < 4) | (lane > nz - 5)

    def final(c, carry):
        each(c, 0, xp_ref, xl_ref, 3)
        each(c, 1, xn_ref, xr_ref, 3)
        i_copy(c).wait()
        r = rows(c)
        packed = pd_ref[r, :]
        for x in range(nx):
            strip = jnp.where(edge, pltpu.roll(packed, (128 - 4 - 8 * x) % 128, 1), 0.0)
            v = o_s[x, r, :] + strip
            if x < 4:
                v = v + add_s[x]
            if x >= nx - 4:
                v = v + add_s[x - nx + 8]
            o_s[x, r, :] = v
        o_copy(c).start()
        return carry

    lax.fori_loop(0, chunks, final, 0)
    for x in range(nx):
        rim_ref[0, x] = o_s[x, 0:8, :]
        rim_ref[1, x] = o_s[x, ny - 8 : ny, :]
    for c in range(chunks):
        o_copy(c).wait()


def join(out, packed, x_prev, x_next, x_left, x_right, e1, d):
    nx, ny, nz = out.shape
    chunks = ny // CH
    return pl.pallas_call(
        join_kernel,
        out_shape=[sds(nx, ny, nz), sds(2, nx, 8, nz)],
        in_specs=[HBM] + [VMEM] * 6 + [HBM],
        out_specs=[HBM, VMEM],
        scratch_shapes=[
            pltpu.VMEM((nx, ny, nz), F32),
            pltpu.VMEM((18, ny + 16, nz), F32),
            pltpu.VMEM((8, CH, nz), F32),
            pltpu.VMEM((4, ny, nz), F32),
            pltpu.SemaphoreType.DMA((chunks,)),
            pltpu.SemaphoreType.DMA((chunks,)),
            pltpu.SemaphoreType.DMA((4,)),
        ],
        input_output_aliases={0: 0},
        compiler_params=params(26),
        cost_estimate=cost(9),
    )(out, packed, x_prev, x_next, x_left, x_right, e1, d)


def finish_kernel(o_hbm, rim_ref, w_ref, wp_ref, wn_ref, l_ref, r_ref, gw_ref, gr_ref, out_hbm, new_s, sem):
    lane = lax.broadcasted_iota(jnp.int32, (24, 128), 1)
    half = lax.broadcasted_iota(jnp.int32, (8, 128), 0)
    ny = out_hbm.shape[1]
    copies = []
    for wall in range(2):
        at = wall * 16

        def rows(mine, before, after):
            return jnp.concatenate([mine, jnp.where(half < 4, after[0:8], before[8:16])], axis=0)

        def take(ref, base):
            return ref[base + at : base + at + 16, :]

        centre = rows(take(w_ref, 0), take(wp_ref, 0), take(wn_ref, 0))
        left = rows(take(l_ref, 0), take(l_ref, 32), take(l_ref, 64))
        right = rows(take(r_ref, 0), take(r_ref, 32), take(r_ref, 64))
        beyond = jnp.where(lane < 3, right, jnp.where(lane > 124, left, 0.0))
        w = jnp.concatenate([centre, beyond], axis=1)
        g = []
        for j in range(4):
            mine = gr_ref[wall, :, j if wall == 0 else 7 - j, :]
            halo = gw_ref[wall, j]
            g.append(jnp.concatenate([jnp.concatenate([mine, halo[16:24, 0:128]], axis=0), halo[:, 128:256]], axis=1))

        def xz(v):
            return pltpu.roll(v, 1, 0) + pltpu.roll(v, 23, 0) + pltpu.roll(v, 1, 1) + pltpu.roll(v, 255, 1)

        e0 = g[0] * w
        a0 = 1.2 * e0 + g[0] * xz(e0)
        a1 = g[1] * e0
        b0 = 0.2 * a0 + e0 + g[0] * (a1 + xz(a0))
        b1 = 0.2 * a1 + g[1] * (a0 + xz(a1))
        b2 = g[2] * a1
        c0 = 0.2 * b0 + e0 + g[0] * (b1 + xz(b0))
        c1 = 0.2 * b1 + g[1] * (b0 + b2 + xz(b1))
        c2 = 0.2 * b2 + g[2] * (b1 + xz(b2))
        c3 = g[3] * b2
        new_s[wall] = rim_ref[wall]
        for j, v in enumerate((c0, c1, c2, c3)):
            y = j if wall == 0 else 7 - j
            new_s[wall, :, y, :] = new_s[wall, :, y, :] + v[0:16, 0:128]
        first = 0 if wall == 0 else ny - 8
        copies.append(pltpu.make_async_copy(new_s.at[wall], out_hbm.at[:, first : first + 8, :], sem.at[wall]))
        copies[wall].start()
    for copy in copies:
        copy.wait()


def finish(out, edge_rows, w, w_prev, w_next, left, right, gw, g_rows):
    nx, ny, nz = out.shape
    return pl.pallas_call(
        finish_kernel,
        out_shape=sds(nx, ny, nz),
        in_specs=[HBM] + [VMEM] * 8,
        out_specs=HBM,
        scratch_shapes=[pltpu.VMEM((2, nx, 8, nz), F32), pltpu.SemaphoreType.DMA((2,))],
        input_output_aliases={0: 0},
        compiler_params=params(8),
        cost_estimate=cost(2),
    )(out, edge_rows, w, w_prev, w_next, left, right, gw, g_rows)


def trio_kernel(a_ref, b_ref, c_ref, out_ref):
    for k, ref in enumerate((a_ref, b_ref, c_ref)):
        out_ref[k * 32 : k * 32 + 32, :] = ref[...]


def trio_of(a, b, c):
    return pl.pallas_call(trio_kernel, out_shape=sds(96, 128), in_specs=[VMEM] * 3, out_specs=VMEM, compiler_params=params(4), cost_estimate=cost(1))(a, b, c)


def shift(block, axis, distance):
    size = lax.axis_size(axis)
    return lax.ppermute(block, axis, [((i - distance) % size, i) for i in range(size)])


def local(right_side, pressure, diagonal, corrections, wall_cells, owners):
    n_dev = lax.axis_size("gx") * lax.axis_size("gz")
    zl, zr, dx, x_left, x_right = edges(pressure, right_side, diagonal)
    corrections, x_left = lax.optimization_barrier((corrections, x_left))
    slots = pack(corrections, wall_cells, owners, n_dev)
    got = lax.all_to_all(slots.reshape(n_dev, 8, 128), AXES, split_axis=0, concat_axis=0, tiled=True).reshape(n_dev * 8, 128)
    x_prev = shift(x_right, "gx", 1)
    x_next = shift(x_left, "gx", -1)
    out, e1, g_rows = main_part(pressure, right_side, diagonal, x_left)
    x_prev, x_next, e1 = lax.optimization_barrier((x_prev, x_next, e1))
    zl, zr = relay(zl, zr, x_prev, x_next)
    far_l = shift(zr, "gz", 1)
    far_r = shift(zl, "gz", -1)
    w = wall_sums(got)
    w_prev = shift(w, "gx", 1)
    w_next = shift(w, "gx", -1)
    packed, gw = strips(zl, zr, dx, far_l, far_r, x_prev, x_next)
    w_prev, w_next, packed = lax.optimization_barrier((w_prev, w_next, packed))
    trio = trio_of(w, w_prev, w_next)
    left = shift(trio, "gz", 1)
    right = shift(trio, "gz", -1)
    out, edge_rows = join(out, packed, x_prev, x_next, x_left, x_right, e1, diagonal)
    return finish(out, edge_rows, w, w_prev, w_next, left, right, gw, g_rows)


def solution(mesh):
    in_specs = (
        P("gx", None, "gz"),
        P("gx", None, "gz"),
        P("gx", None, "gz"),
        P(AXES, None),
        P(AXES, None),
        P(AXES, None),
    )
    return jax.shard_map(local, mesh=mesh, in_specs=in_specs, out_specs=P("gx", None, "gz"), check_vma=False)
```
